512 devices in a mesh: gx: 16 (over z_hi, y), gy: 32 (over z_lo, x, core).
Axes of the slice: x: 4, y: 8, z: 8 (z_hi: 2, z_lo: 4; z = z_hi * 4 + z_lo), core: 2. Of those that a mesh axis runs over, the one named last changes fastest.
Arguments:
- intensities: int32 [384, 256, 128], P('gx', 'gy'), may hold values from 0 to 255
- labels: int32 [384, 256, 128], P('gx', 'gy'), may hold values from 0 to 2
Outputs:
- solution: float32 [384, 256, 128], P('gx', 'gy')
The draws below stay inside these ranges and needn't reach their ends.
All inputs are finite; a program needn't handle non-finite values.
Results may differ from the reference program's by a relative error of at most 0.0001.
Values sent between devices are 32-bit elements; how exact they have to be, the bound alone decides.
A program may use at most 64 MiB of HBM per device.

```python
import jax
import jax.numpy as jnp
from jax import lax

COARSE_ITERS = 30
NX = 384
NY = 256
NZ = 128


def draw_intensities(key, part):
    key = jax.random.fold_in(key, 11)
    subkeys = jax.random.split(key, 5)
    region_span = 12
    region_cells = (NX // region_span + 2, NY // region_span + 2, NZ // region_span + 2)
    bright = jax.random.randint(subkeys[0], region_cells, 0, 2)
    level_low = jax.random.randint(subkeys[1], region_cells, 0, 64)
    level_high = jax.random.randint(subkeys[2], region_cells, 192, 256)
    region_level = jnp.where(bright == 1, level_high, level_low)
    shifts = jax.random.randint(subkeys[3], (3,), 0, region_span)
    index_x = (jnp.arange(NX, dtype=jnp.int32) + shifts[0]) // region_span
    index_y = (jnp.arange(NY, dtype=jnp.int32) + shifts[1]) // region_span
    index_z = (jnp.arange(NZ, dtype=jnp.int32) + shifts[2]) // region_span
    base_level = region_level[index_x[:, None, None], index_y[None, :, None], index_z[None, None, :]]
    jitter = jax.random.randint(subkeys[4], (NX, NY, NZ), -40, 41)
    return jnp.clip(base_level + jitter, 0, 255).astype(jnp.int32)


def draw_labels(key, part):
    key = jax.random.fold_in(key, 23)
    subkeys = jax.random.split(key, 2)
    cell_span = 8
    seed_cells = (NX // cell_span + 2, NY // cell_span + 2, NZ // cell_span + 2)
    codes = jax.random.randint(subkeys[0], seed_cells, 0, 1029)
    shifts = jax.random.randint(subkeys[1], (3,), 0, cell_span)
    place_x = jnp.arange(NX, dtype=jnp.int32) + shifts[0]
    place_y = jnp.arange(NY, dtype=jnp.int32) + shifts[1]
    place_z = jnp.arange(NZ, dtype=jnp.int32) + shifts[2]
    code_full = codes[(place_x // cell_span)[:, None, None], (place_y // cell_span)[None, :, None], (place_z // cell_span)[None, None, :]]
    seed_kind = code_full // 343
    corner = code_full % 343
    delta_x = (place_x % cell_span)[:, None, None] - corner // 49
    delta_y = (place_y % cell_span)[None, :, None] - corner // 7 % 7
    delta_z = (place_z % cell_span)[None, None, :] - corner % 7
    inside = (delta_x >= 0) & (delta_x <= 1) & (delta_y >= 0) & (delta_y <= 1) & (delta_z >= 0) & (delta_z <= 1)
    return jnp.where(inside, seed_kind, 0).astype(jnp.int32)


def setup_inputs(seed: int = 0) -> dict:
    key_list = jax.random.split(jax.random.key(seed), 3)
    intensities = draw_intensities(jax.random.fold_in(key_list[2], 71), 0)
    labels = draw_labels(jax.random.fold_in(key_list[2], 71), 0)
    return dict(intensities=intensities, labels=labels)


edge_beta = 3.0
seed_gamma = 4.0
base_mass = 0.1
damping = 0.7


def edge_weight(upper, lower):
    scaled = (upper - lower) / 255.0
    return jnp.exp(-edge_beta * scaled * scaled)


def pad_axis(array, axis, before, after):
    widths = [(0, 0), (0, 0), (0, 0)]
    widths[axis] = (before, after)
    return jnp.pad(array, widths)


def coarsen_operator(operator):
    plus_x, minus_x, plus_y, minus_y, plus_z, minus_z, mass_term = operator

    def blocks(array):
        size_a, size_b, size_c = array.shape
        return array.reshape(size_a // 2, 2, size_b // 2, 2, size_c // 2, 2)

    return (blocks(plus_x)[:, 1].sum(axis=(2, 4)), blocks(minus_x)[:, 0].sum(axis=(2, 4)),
            blocks(plus_y)[:, :, :, 1].sum(axis=(1, 4)), blocks(minus_y)[:, :, :, 0].sum(axis=(1, 4)),
            blocks(plus_z)[:, :, :, :, :, 1].sum(axis=(1, 3)), blocks(minus_z)[:, :, :, :, :, 0].sum(axis=(1, 3)),
            blocks(mass_term).sum(axis=(1, 3, 5)))


def restrict_field(field):
    size_a, size_b, size_c = field.shape
    return field.reshape(size_a // 2, 2, size_b // 2, 2, size_c // 2, 2).sum(axis=(1, 3, 5))


def prolong_field(field):
    size_a, size_b, size_c = field.shape
    spread = jnp.broadcast_to(field[:, None, :, None, :, None], (size_a, 2, size_b, 2, size_c, 2))
    return spread.reshape(size_a * 2, size_b * 2, size_c * 2)


def diagonal_of(operator):
    plus_x, minus_x, plus_y, minus_y, plus_z, minus_z, mass_term = operator
    return mass_term + plus_x + minus_x + plus_y + minus_y + plus_z + minus_z


def apply_operator(padded, operator):
    plus_x, minus_x, plus_y, minus_y, plus_z, minus_z, mass_term = operator
    center = padded[1:-1, 1:-1]
    zpadded = jnp.pad(center, ((0, 0), (0, 0), (1, 1)))
    result = mass_term * center
    result = result + plus_x * (center - padded[2:, 1:-1]) + minus_x * (center - padded[:-2, 1:-1])
    result = result + plus_y * (center - padded[1:-1, 2:]) + minus_y * (center - padded[1:-1, :-2])
    result = result + plus_z * (center - zpadded[:, :, 2:]) + minus_z * (center - zpadded[:, :, :-2])
    return result


def relax(field, padded, rhs, operator, diagonal):
    return field + damping * (rhs - apply_operator(padded, operator)) / diagonal


def side_pad(field):
    return jnp.pad(field, ((1, 1), (1, 1), (0, 0)))


def fine_operator(intensities, labels):
    values = intensities.astype(jnp.float32)
    parts = []
    for axis in range(3):
        count = values.shape[axis]
        weights = edge_weight(lax.slice_in_dim(values, 1, count, axis=axis), lax.slice_in_dim(values, 0, count - 1, axis=axis))
        parts.append(pad_axis(weights, axis, 0, 1))
        parts.append(pad_axis(weights, axis, 1, 0))
    mass_term = (base_mass + jnp.where(labels > 0, seed_gamma, 0.0)).astype(jnp.float32)
    rhs = jnp.where(labels == 1, seed_gamma, 0.0).astype(jnp.float32)
    return tuple(parts) + (mass_term,), rhs


def reference(intensities, labels):
    operator, rhs = fine_operator(intensities, labels)
    operators = [operator]
    for level in range(3):
        operators.append(coarsen_operator(operators[-1]))

    def cycle(level, source):
        current = operators[level]
        diagonal = diagonal_of(current)
        field = damping * source / diagonal
        if level == 3:
            def turn(index, state):
                return relax(state, side_pad(state), source, current, diagonal)
            return lax.fori_loop(1, COARSE_ITERS, turn, field)
        field = relax(field, side_pad(field), source, current, diagonal)
        residual = source - apply_operator(side_pad(field), current)
        field = field + prolong_field(cycle(level + 1, restrict_field(residual)))
        field = relax(field, side_pad(field), source, current, diagonal)
        field = relax(field, side_pad(field), source, current, diagonal)
        return field

    return cycle(0, rhs)
```

```python
import jax
import jax.numpy as jnp
from jax import lax
from jax.experimental import pallas as pl
from jax.experimental.pallas import tpu as pltpu
from jax.sharding import PartitionSpec as P

COARSE_ITERS = 30

edge_beta = 3.0
seed_gamma = 4.0
base_mass = 0.1
damping = 0.7

MESH = pl.DeviceIdType.MESH
f32 = jnp.float32

BX, BY, BZ = 24, 8, 128
GX, GY = 16, 32

NEAR = [(dx, dy) for dx in (-1, 0, 1) for dy in (-1, 0, 1) if (dx, dy) != (0, 0)]
WIDE = [(dx, dy) for dx in (-1, 0, 1) for dy in range(-3, 4) if (dx, dy) != (0, 0)]


def place(shape, axis):
    return lax.broadcasted_iota(jnp.int32, shape, axis)


def up(array, distance, axis):
    return pltpu.roll(array, array.shape[axis] - distance, axis)


def down(array, distance, axis):
    return pltpu.roll(array, distance, axis)


def odd(array, distance, axis):
    return (place(array.shape, axis) // distance) % 2 == 1


def high(array, distance, axis):
    return jnp.where(odd(array, distance, axis), array, up(array, distance, axis))


def low(array, distance, axis):
    return jnp.where(odd(array, distance, axis), down(array, distance, axis), array)


def pair(array, distance, axis):
    return array + jnp.where(
        odd(array, distance, axis), down(array, distance, axis), up(array, distance, axis)
    )


def halves(array):
    split = array.reshape((array.shape[0] // 2, 2) + array.shape[1:])
    return split[:, 0], split[:, 1]


def pair_x(array):
    first, second = halves(array)
    return first + second


def coarsen(operator, distance):
    px, py, my, pz, mass = operator
    next_px = jnp.concatenate([px[0:1], halves(px[1:])[1]], axis=0)
    next_px = pair(pair(next_px, distance, 1), distance, 2)
    next_py = high(pair(pair_x(py), distance, 2), distance, 1)
    next_my = low(pair(pair_x(my), distance, 2), distance, 1)
    next_pz = high(pair(pair_x(pz), distance, 1), distance, 2)
    next_mass = pair(pair(pair_x(mass), distance, 1), distance, 2)
    return next_px, next_py, next_my, next_pz, next_mass


def own_diagonal(operator, distance):
    px, py, my, pz, mass = operator
    return mass + px[1:] + px[:-1] + py + my + pz + down(pz, distance, 2)


def weight(upper, lower):
    gap = upper - lower
    return jnp.exp(gap * gap * (-edge_beta / (255.0 * 255.0)))


def step(source, first, count, weights, rhs, dist_y, dist_z, rows=None):
    v = source[pl.ds(first - 1, count + 2)]
    c = v[1:-1]
    near = [v[2:], v[:-2], up(c, dist_y, 1), down(c, dist_y, 1), up(c, dist_z, 2), down(c, dist_z, 2)]
    rows = c.shape[1] if rows is None else rows
    here = c[:, :rows]
    total = (1.0 - damping) * here + rhs[pl.ds(first, count), 0:rows, :]
    for w, n in zip(weights, near):
        total = total + w[pl.ds(first, count), 0:rows, :] * n[:, :rows]
    return here, total


def sweep(source, target, first, last, count, weights, rhs, dist_y, dist_z):
    def turn(index, carry):
        at = first + index * count
        _, total = step(source, at, count, weights, rhs, dist_y, dist_z)
        target[pl.ds(at, count)] = total
        return carry

    lax.fori_loop(0, (last + 1 - first) // count, turn, 0)


def normalise(px, px_before, py, my, pz, mz, mass, stores, at, count):
    diagonal = mass + px + px_before + py + my + pz + mz
    scale = damping / diagonal
    for store, value in zip(stores, (px, px_before, py, my, pz, mz)):
        store[pl.ds(at, count)] = value * scale
    return diagonal, scale


def all_bytes(ref, sem):
    pltpu.make_async_copy(ref, ref, sem).wait()


def kernel(
    ints, labels, out,
    ibuf, lbuf, w0, b0, d0, fine, va0, vb0,
    p1, b1, w1, d1, va1, vb1,
    p2, b2, w2, d2, va2, vb2,
    o3, g1o, q6o, g2o, s3, g1, q6, g2, w3, solved,
    local_sem, send_sem, recv_sem,
):
    gx, gy = lax.axis_index("gx"), lax.axis_index("gy")

    def device(dx, dy):
        return (lax.rem(gx + dx + GX, GX), lax.rem(gy + dy + GY, GY))

    def send(source, target, which, dx, dy):
        pltpu.make_async_remote_copy(
            source, target, send_sem.at[which], recv_sem.at[which],
            device_id=device(dx, dy), device_id_type=MESH,
        ).start()

    own_i = pltpu.make_async_copy(ints, ibuf.at[4:28, 0:8], local_sem.at[0])
    own_l = pltpu.make_async_copy(labels, lbuf.at[4:28, 0:8], local_sem.at[1])
    own_i.start()
    own_l.start()
    p2[:, 8:10, :] = jnp.ones((18, 2, BZ), f32)
    b2[:, 8:10, :] = jnp.zeros((18, 2, BZ), f32)
    barrier = pltpu.get_barrier_semaphore()

    def greet(dx, dy):
        pl.semaphore_signal(barrier, inc=1, device_id=device(dx, dy), device_id_type=MESH)

    def greet_x(dx, carry):
        greet(dx, 0)
        return carry

    def greet_y(dy, carry):
        greet(0, dy)
        return carry

    for dx, dy in WIDE:
        if dx and dy:
            greet(dx, dy)
    lax.fori_loop(1, GX, greet_x, 0)
    lax.fori_loop(1, GY, greet_y, 0)
    pl.semaphore_wait(barrier, 12 + (GX - 1) + (GY - 1))

    for dx, dy in NEAR:
        sx, tx = {1: (pl.ds(20, 4), pl.ds(0, 4)), -1: (pl.ds(0, 4), pl.ds(28, 4)), 0: (pl.ds(0, 24), pl.ds(4, 24))}[dx]
        sy, ty = {1: (pl.ds(4, 4), pl.ds(12, 4)), -1: (pl.ds(0, 4), pl.ds(8, 4)), 0: (pl.ds(0, 8), pl.ds(0, 8))}[dy]
        send(ints.at[sx, sy], ibuf.at[tx, ty], 0, dx, dy)
        send(labels.at[sx, sy], lbuf.at[tx, ty], 1, dx, dy)
    own_i.wait()
    own_l.wait()
    all_bytes(ibuf.at[0:20], recv_sem.at[0])
    all_bytes(lbuf.at[0:20], recv_sem.at[1])

    count = 5

    def fine_turn(index, carry):
        at = 1 + index * count
        wide = ibuf[pl.ds(at - 1, count + 2)].astype(f32)
        lab = lbuf[pl.ds(at, count)]
        c = wide[1:-1]
        px = weight(wide[1:], wide[:-1])
        gone_x = gx * BX + (at - 5) + place(px.shape, 0)
        px = jnp.where((gone_x == GX * BX - 1) | (gone_x == -1), 0.0, px)
        row = place(c.shape, 1)
        gone_y = gy * BY + jnp.where(row >= 12, row - 16, row)
        py = jnp.where((gone_y == GY * BY - 1) | (gone_y == -1), 0.0, weight(up(c, 1, 1), c))
        my = down(py, 1, 1)
        pz = jnp.where(place(c.shape, 2) == BZ - 1, 0.0, weight(up(c, 1, 2), c))
        mz = down(pz, 1, 2)
        mass = base_mass + jnp.where(lab > 0, seed_gamma, 0.0)
        diagonal, scale = normalise(px[1:], px[:-1], py, my, pz, mz, mass, w0, at, count)
        b0[pl.ds(at, count)] = jnp.where(lab == 1, seed_gamma, 0.0) * scale
        d0[pl.ds(at, count)] = diagonal[:, 0:8] * (1.0 / damping)
        for slot, value in enumerate((px[1:], py, my, pz, mass)):
            fine[slot, pl.ds(at, count)] = value[:, 0:8]
        return carry

    lax.fori_loop(0, 30 // count, fine_turn, 0)

    op1 = coarsen(
        (fine[0, 3:28], fine[1, 4:28], fine[2, 4:28], fine[3, 4:28], fine[4, 4:28]), 1
    )
    px, py, _, pz, mass = op1
    ybit, zbit = odd(py, 1, 1), odd(py, 1, 2)
    p1[4:16, 0:8, :] = jnp.where(ybit, jnp.where(zbit, mass, pz), jnp.where(zbit, py, px[1:]))

    def send_1(ref, which):
        for dx, dy in NEAR:
            sx, tx = {1: (pl.ds(12, 4), pl.ds(0, 4)), -1: (pl.ds(4, 4), pl.ds(16, 4)), 0: (pl.ds(4, 12), pl.ds(4, 12))}[dx]
            ty = pl.ds({1: 16, -1: 8, 0: 0}[dy], 8)
            send(ref.at[sx, pl.ds(0, 8)], ref.at[tx, ty], which, dx, dy)

    send_1(p1, 2)

    sweep(b0, va0, 2, 29, 4, w0, b0, 1, 1)

    scale1 = damping / own_diagonal(op1, 2)
    d1[...] = scale1

    def residual_0(index, carry):
        at = 4 + 8 * index
        here, total = step(va0, at, 8, w0, b0, 1, 1, 8)
        r = pair_x(d0[pl.ds(at, 8)] * (total - here))
        r = pair(pair(r, 1, 1), 1, 2)
        b1[pl.ds(4 + 4 * index, 4), 0:8, :] = r * d1[pl.ds(4 * index, 4)]
        return carry

    lax.fori_loop(0, 3, residual_0, 0)
    send_1(b1, 3)

    op2 = coarsen(op1, 2)
    scale2 = damping / own_diagonal(op2, 4)
    d2[...] = scale2
    px, py, _, pz, mass = op2
    slot = place(py.shape, 2) % 4

    def compact(array):
        return jnp.where(place(array.shape, 1) == 0, array, up(array, 3, 1))[:, 0:2]

    p2[6:12, 0:2, :] = compact(
        jnp.where(slot == 0, px[1:], jnp.where(slot == 1, py, jnp.where(slot == 2, pz, mass)))
    )

    def send_2(ref, which):
        for dx, dy in WIDE:
            send(
                ref.at[6:12, 0:2], ref.at[pl.ds(6 * (1 - dx), 6), pl.ds((-2 * dy) % 16, 2)],
                which, dx, dy,
            )

    send_2(p2, 4)

    op3 = coarsen(op2, 4)
    scale3 = damping / own_diagonal(op3, 8)
    px, py, _, pz, mass = op3
    for index, value in enumerate((px[1:], py, pz, mass)):
        o3[3 * index : 3 * index + 3] = value
    g1o[:, pl.ds(gx, 1), :] = o3[:, 0:1, :]

    def gather_x(source, target, which):
        def turn(dx, carry):
            send(source.at[:, 0:1], target.at[:, pl.ds(gx, 1)], which, dx, 0)
            return carry

        lax.fori_loop(1, GX, turn, 0)

    seat = (gy % 4) * 8 + gy // 4

    def gather_y(source, target, which):
        def turn(dy, carry):
            send(source.at[:, 0:1], target.at[:, pl.ds(seat, 1)], which, 0, dy)
            return carry

        target[:, pl.ds(seat, 1), :] = source[:, 0:1, :]
        lax.fori_loop(1, GY, turn, 0)

    def merge_x(source, target, kinds):
        for kind in range(kinds):
            rows = source[3 * kind : 3 * kind + 3]
            mine = place(rows.shape, 2) % 8 == place(rows.shape, 1) // 2
            kept = jnp.where(mine, rows, 0.0)
            kept = kept[:, 0:8] + kept[:, 8:16]
            kept = kept + up(kept, 2, 1)
            kept = kept + up(kept, 4, 1)
            target[6 * kind : 6 * kind + 3] = kept
            target[6 * kind + 3 : 6 * kind + 6] = up(kept, 1, 1)

    gather_x(o3, g1o, 6)

    all_bytes(p1.at[0:16], recv_sem.at[2])

    def weights_1(index, carry):
        at = 1 + 3 * index
        packed = p1[pl.ds(at - 1, 4)]
        even_z, odd_z = low(packed, 1, 2), high(packed[1:], 1, 2)
        px, pz = low(even_z, 1, 1), high(even_z[1:], 1, 1)
        py, mass = low(odd_z, 1, 1), high(odd_z, 1, 1)
        diagonal, _ = normalise(px[1:], px[:-1], py, down(py, 2, 1), pz, down(pz, 2, 2), mass, w1, at, 3)
        va1[pl.ds(at, 3)] = diagonal * (1.0 / damping)
        return carry

    lax.fori_loop(0, 6, weights_1, 0)
    d1[...] = va1[4:16, 0:8, :]
    all_bytes(b1.at[0:16], recv_sem.at[3])
    sweep(b1, va1, 1, 18, 3, w1, b1, 2, 2)

    def residual_1(index, carry):
        at = 4 + 4 * index
        here, total = step(va1, at, 4, w1, b1, 2, 2, 8)
        r = pair_x(d1[pl.ds(4 * index, 4)] * (total - here))
        r = pair(pair(r, 2, 1), 2, 2)
        b2[pl.ds(6 + 2 * index, 2), 0:2, :] = compact(r * d2[pl.ds(2 * index, 2)])
        return carry

    lax.fori_loop(0, 3, residual_1, 0)
    send_2(b2, 5)

    all_bytes(p2.at[0:15], recv_sem.at[4])

    def weights_2(index, carry):
        at = 1 + 4 * index
        packed = p2[pl.ds(at - 1, 5)]
        even_z, odd_z = low(packed, 1, 2), high(packed[1:], 1, 2)
        px, pz = low(even_z, 2, 2), high(even_z[1:], 2, 2)
        py, mass = low(odd_z, 2, 2), high(odd_z, 2, 2)
        diagonal, _ = normalise(px[1:], px[:-1], py, down(py, 1, 1), pz, down(pz, 4, 2), mass, w2, at, 4)
        vb2[pl.ds(at, 4)] = diagonal * (1.0 / damping)
        return carry

    lax.fori_loop(0, 4, weights_2, 0)
    all_bytes(g1o.at[:, 0:15], recv_sem.at[6])
    merge_x(g1o, q6o, 4)
    gather_y(q6o, g2o, 7)

    all_bytes(b2.at[0:15], recv_sem.at[5])
    sweep(b2, va2, 2, 15, 2, w2, b2, 1, 4)
    here, total = step(va2, 6, 6, w2, b2, 1, 4, 8)
    r = pair_x(vb2[6:12, 0:8, :] * (total - here))
    r = pair(pair(r, 1, 1), 4, 2)
    s3[...] = r * scale3
    g1[:, pl.ds(gx, 1), :] = s3[:, 0:1, :]
    gather_x(s3, g1, 8)

    whole = (6, 4, 8, BZ)
    all_bytes(g2o.at[:, 0:31], recv_sem.at[7])
    px, py, pz, mass = [g2o[6 * k : 6 * k + 6].reshape(whole) for k in range(4)]

    def up_x(v):
        return jnp.concatenate([v[1:], up(v[0], 1, 2)[None]], axis=0)

    def down_x(v):
        return jnp.concatenate([down(v[5], 1, 2)[None], v[:5]], axis=0)

    def up_y(v):
        return jnp.concatenate([v[:, 1:], up(v[:, 0], 1, 1)[:, None]], axis=1)

    def down_y(v):
        return jnp.concatenate([down(v[:, 3], 1, 1)[:, None], v[:, :3]], axis=1)

    def lanes(v, shift):
        return pltpu.roll(v.reshape(24, 8, BZ), shift, 2).reshape(whole)

    mx, my, mz = down_x(px), down_y(py), lanes(pz, 8)
    scale = damping / (mass + px + mx + py + my + pz + mz)
    for index, value in enumerate((px, mx, py, my, pz, mz)):
        w3[index] = value * scale

    all_bytes(g1.at[:, 0:15], recv_sem.at[8])
    merge_x(g1, q6, 1)
    gather_y(q6, g2, 9)
    all_bytes(g2.at[:, 0:31], recv_sem.at[9])
    source = g2[...].reshape(whole)

    def solve(index, v):
        near = (up_x(v), down_x(v), up_y(v), down_y(v), lanes(v, BZ - 8), lanes(v, 8))
        total = (1.0 - damping) * v + g2[...].reshape(whole)
        for k, n in enumerate(near):
            total = total + w3[k] * n
        return total

    solved[...] = lax.fori_loop(1, COARSE_ITERS, solve, source).reshape(6, 32, BZ)

    row = (place((16, BZ), 0) // 2 + 2) % 8
    slot = place((16, BZ), 1) % 8
    for j in range(-2, 5):
        at = lax.rem(3 * gx + j + 48, 48)
        tile = jnp.zeros((16, BZ), f32)
        for k in range(-2, 3):
            y = lax.rem(gy + k + GY, GY)
            line = solved[pl.ds(lax.rem(at, 6), 1), pl.ds((y % 4) * 8 + y // 4, 1), :]
            tile = jnp.where(row == k + 2, line.reshape(1, BZ), tile)
        tile = jnp.where(slot == at // 6, tile, 0.0)
        tile = pair(pair(pair(tile, 1, 1), 2, 1), 4, 1)
        va2[6 + 2 * j : 8 + 2 * j] = va2[6 + 2 * j : 8 + 2 * j] + tile[None]
    sweep(va2, vb2, 3, 14, 2, w2, b2, 1, 4)
    sweep(vb2, va2, 4, 13, 2, w2, b2, 1, 4)

    upper = place((1, 8, BZ), 1) >= 4

    def correct_1(index, carry):
        from_plane = 4 + index
        at = 1 + 2 * index - 1
        tiles = []
        for first in (0, 2, 14):
            a = va2[pl.ds(from_plane, 1), first : first + 1, :]
            b = va2[pl.ds(from_plane, 1), first + 1 : first + 2, :]
            tiles.append(jnp.where(upper, b, a))
        whole_row = jnp.concatenate(tiles, axis=1)
        va1[pl.ds(at, 2)] = va1[pl.ds(at, 2)] + whole_row
        return carry

    lax.fori_loop(0, 10, correct_1, 0)
    sweep(va1, vb1, 2, 17, 2, w1, b1, 2, 2)
    sweep(vb1, va1, 3, 16, 2, w1, b1, 2, 2)

    def correct_0(index, carry):
        at = 2 + 2 * index
        coarse = va1[pl.ds(3 + index, 1)]
        whole_row = jnp.concatenate(
            [coarse[:, 0:8], jnp.where(upper, coarse[:, 16:24], coarse[:, 8:16])], axis=1
        )
        va0[pl.ds(at, 2)] = va0[pl.ds(at, 2)] + whole_row
        return carry

    lax.fori_loop(0, 14, correct_0, 0)
    sweep(va0, vb0, 2, 29, 4, w0, b0, 1, 1)

    def finish(index, carry):
        at = 4 + 4 * index
        _, total = step(vb0, at, 4, w0, b0, 1, 1, 8)
        out[pl.ds(4 * index, 4)] = total
        return carry

    lax.fori_loop(0, 6, finish, 0)

    for which, ref in enumerate(
        (ibuf.at[0:20], lbuf.at[0:20], p1.at[0:16], b1.at[0:16], p2.at[0:15], b2.at[0:15],
         g1o.at[:, 0:15], g2o.at[:, 0:31], g1.at[:, 0:15], g2.at[:, 0:31])
    ):
        all_bytes(ref, send_sem.at[which])


def shards(intensities, labels):
    def vmem(*shape, dtype=f32):
        return pltpu.VMEM(shape, dtype)

    fine_shape, one, two = (32, 16, BZ), (20, 24, BZ), (18, 16, BZ)
    return pl.pallas_call(
        kernel,
        out_shape=jax.ShapeDtypeStruct((BX, BY, BZ), f32),
        in_specs=[pl.BlockSpec(memory_space=pl.ANY)] * 2,
        out_specs=pl.BlockSpec(memory_space=pltpu.VMEM),
        scratch_shapes=[
            vmem(*fine_shape, dtype=jnp.int32), vmem(*fine_shape, dtype=jnp.int32),
            [vmem(*fine_shape)] * 6, vmem(*fine_shape), vmem(32, 8, BZ), vmem(5, 32, 8, BZ),
            vmem(*fine_shape), vmem(*fine_shape),
            vmem(*one), vmem(*one), [vmem(*one)] * 6, vmem(12, 8, BZ), vmem(*one), vmem(*one),
            vmem(*two), vmem(*two), [vmem(*two)] * 6, vmem(6, 8, BZ), vmem(*two), vmem(*two),
            vmem(12, 8, BZ), vmem(12, 16, BZ), vmem(24, 8, BZ), vmem(24, 32, BZ),
            vmem(3, 8, BZ), vmem(3, 16, BZ), vmem(6, 8, BZ), vmem(6, 32, BZ),
            vmem(6, 6, 4, 8, BZ), vmem(6, 32, BZ),
            pltpu.SemaphoreType.DMA((2,)),
            pltpu.SemaphoreType.DMA((10,)),
            pltpu.SemaphoreType.DMA((10,)),
        ],
        compiler_params=pltpu.CompilerParams(
            collective_id=0, has_side_effects=True, vmem_limit_bytes=40 * 1024 * 1024
        ),
        name="v_cycle",
    )(intensities, labels)


def solution(mesh):
    return jax.shard_map(
        shards,
        mesh=mesh,
        in_specs=(P("gx", "gy", None), P("gx", "gy", None)),
        out_specs=P("gx", "gy", None),
        check_vma=False,
    )
```

```python
import jax
import jax.numpy as jnp
from jax import lax
from jax.experimental import pallas as pl
from jax.experimental.pallas import tpu as pltpu
from jax.sharding import PartitionSpec as P

COARSE_ITERS = 30

edge_beta = 3.0
seed_gamma = 4.0
base_mass = 0.1
damping = 0.7

MESH = pl.DeviceIdType.MESH
f32 = jnp.float32

BX, BY, BZ = 24, 8, 128
GX, GY = 16, 32

NEAR = [(dx, dy) for dx in (-1, 0, 1) for dy in (-1, 0, 1) if (dx, dy) != (0, 0)]
MIDDLE = [(dx, dy) for dx in (-1, 1, 0) for dy in (0, -1, 1, -2, 2) if (dx, dy) != (0, 0)]


def place(shape, axis):
    return lax.broadcasted_iota(jnp.int32, shape, axis)


def up(array, distance, axis):
    return pltpu.roll(array, array.shape[axis] - distance, axis)


def down(array, distance, axis):
    return pltpu.roll(array, distance, axis)


def odd(array, distance, axis):
    return (place(array.shape, axis) // distance) % 2 == 1


def high(array, distance, axis):
    return jnp.where(odd(array, distance, axis), array, up(array, distance, axis))


def low(array, distance, axis):
    return jnp.where(odd(array, distance, axis), down(array, distance, axis), array)


def pair(array, distance, axis):
    return array + jnp.where(
        odd(array, distance, axis), down(array, distance, axis), up(array, distance, axis)
    )


def halves(array):
    split = array.reshape((array.shape[0] // 2, 2) + array.shape[1:])
    return split[:, 0], split[:, 1]


def pair_x(array):
    first, second = halves(array)
    return first + second


def coarsen(operator, distance):
    px, py, my, pz, mass = operator
    next_px = jnp.concatenate([px[0:1], halves(px[1:])[1]], axis=0)
    next_px = pair(pair(next_px, distance, 1), distance, 2)
    next_py = high(pair(pair_x(py), distance, 2), distance, 1)
    next_my = low(pair(pair_x(my), distance, 2), distance, 1)
    next_pz = high(pair(pair_x(pz), distance, 1), distance, 2)
    next_mass = pair(pair(pair_x(mass), distance, 1), distance, 2)
    return next_px, next_py, next_my, next_pz, next_mass


def own_diagonal(operator, distance):
    px, py, my, pz, mass = operator
    return mass + px[1:] + px[:-1] + py + my + pz + down(pz, distance, 2)


def weight(upper, lower):
    gap = upper - lower
    return jnp.exp(gap * gap * (-edge_beta / (255.0 * 255.0)))


def step(source, first, count, weights, rhs, dist_y, dist_z, rows=None):
    v = source[pl.ds(first - 1, count + 2)]
    c = v[1:-1]
    near = [v[2:], v[:-2], up(c, dist_y, 1), down(c, dist_y, 1), up(c, dist_z, 2), down(c, dist_z, 2)]
    rows = c.shape[1] if rows is None else rows
    here = c[:, :rows]
    total = (1.0 - damping) * here + rhs[pl.ds(first, count), 0:rows, :]
    for w, n in zip(weights, near):
        total = total + w[pl.ds(first, count), 0:rows, :] * n[:, :rows]
    return here, total


def sweep(source, target, first, last, count, weights, rhs, dist_y, dist_z):
    def turn(index, carry):
        at = first + index * count
        _, total = step(source, at, count, weights, rhs, dist_y, dist_z)
        target[pl.ds(at, count)] = total
        return carry

    lax.fori_loop(0, (last + 1 - first) // count, turn, 0, unroll=True)


def normalise(px, px_before, py, my, pz, mz, mass, stores, at, count):
    diagonal = mass + px + px_before + py + my + pz + mz
    scale = damping / diagonal
    for store, value in zip(stores, (px, px_before, py, my, pz, mz)):
        store[pl.ds(at, count)] = value * scale
    return diagonal, scale


def kernel(
    ints, labels, out,
    ibuf, lbuf, w0, b0, d0, fine, va0, vb0,
    p1, b1p, b1, w1, d1, s1, va1, vb1,
    p2, x2, b2, w2, d2, s2, va2, vb2,
    o3, g1o, qo, g2o, o4, g1, q, g2, w3, b3, solved,
    local_sem, send_sem, recv_sem,
):
    gx, gy = lax.axis_index("gx"), lax.axis_index("gy")
    half, chip_y = gx // 8, gx % 8
    chip_z, chip_x, core = half * 4 + gy // 8, gy % 8 // 2, gy % 2
    groups = {}

    def device(dx, dy):
        return (lax.rem(gx + dx + GX, GX), lax.rem(gy + dy + GY, GY))

    def in_plane(k):
        return (half * 8 + (chip_y + k // 2) % 8, gy - core + (core + k) % 2)

    def in_column(k):
        z = (chip_z + k // 4) % 8
        return (z // 4 * 8 + chip_y, z % 4 * 8 + (chip_x + k) % 4 * 2 + core)

    def send(source, target, which, to):
        pltpu.make_async_remote_copy(
            source, target, send_sem.at[which], recv_sem.at[which],
            device_id=to, device_id_type=MESH,
        ).start()

    def each(count, action):
        def turn(index, carry):
            action(index)
            return carry

        lax.fori_loop(1, count, turn, 0)

    def await_bytes(ref, sem):
        pltpu.make_async_copy(ref, ref, sem).wait()

    def arrived(which):
        await_bytes(groups[which], recv_sem.at[which])

    own = [
        pltpu.make_async_copy(ints, ibuf.at[4:28, 0:8], local_sem.at[0]),
        pltpu.make_async_copy(labels, lbuf.at[4:28, 0:8], local_sem.at[1]),
    ]
    for copy in own:
        copy.start()
    barrier = pltpu.get_barrier_semaphore()

    def greet(to):
        pl.semaphore_signal(barrier, inc=1, device_id=to, device_id_type=MESH)

    for dx, dy in MIDDLE:
        greet(device(dx, dy))
    each(16, lambda k: greet(in_plane(k)))
    each(32, lambda k: greet(in_column(k)))
    p2[:, 6:12, :] = jnp.ones((18, 6, BZ), f32)
    x2[:, 6:12, :] = jnp.zeros((18, 6, BZ), f32)
    pl.semaphore_wait(barrier, len(MIDDLE) + 15 + 31)

    def send_inputs(source, target, which, depth, corner_x, corner_y):
        for dx, dy in sorted(NEAR, key=lambda d: (d[0] == 0, d[1] != 0)):
            n, m = (corner_x, corner_y) if dx and dy else (depth, depth)
            sx, tx = {1: (24 - n, 4 - n), -1: (0, 28), 0: (0, 4)}[dx]
            sy, ty = {1: (8 - m, 16 - m), -1: (0, 8), 0: (0, 0)}[dy]
            nx, ny = n if dx else 24, m if dy else 8
            send(
                source.at[sx : sx + nx, sy : sy + ny], target.at[tx : tx + nx, ty : ty + ny],
                which, device(dx, dy),
            )

    send_inputs(ints, ibuf, 0, 4, 3, 4)
    send_inputs(labels, lbuf, 1, 3, 2, 2)
    groups[0] = ibuf.at[0:19]
    groups[1] = lbuf.at[0:13]
    for copy in own:
        copy.wait()
    arrived(0)
    arrived(1)

    count = 5

    def fine_turn(index, carry):
        at = 1 + index * count
        wide = ibuf[pl.ds(at - 1, count + 2)].astype(f32)
        lab = lbuf[pl.ds(at, count)]
        c = wide[1:-1]
        px = weight(wide[1:], wide[:-1])
        gone_x = gx * BX + (at - 5) + place(px.shape, 0)
        px = jnp.where((gone_x == GX * BX - 1) | (gone_x == -1), 0.0, px)
        row = place(c.shape, 1)
        gone_y = gy * BY + jnp.where(row >= 12, row - 16, row)
        py = jnp.where((gone_y == GY * BY - 1) | (gone_y == -1), 0.0, weight(up(c, 1, 1), c))
        my = down(py, 1, 1)
        pz = jnp.where(place(c.shape, 2) == BZ - 1, 0.0, weight(up(c, 1, 2), c))
        mz = down(pz, 1, 2)
        mass = base_mass + jnp.where(lab > 0, seed_gamma, 0.0)
        diagonal, scale = normalise(px[1:], px[:-1], py, my, pz, mz, mass, w0, at, count)
        b0[pl.ds(at, count)] = jnp.where(lab == 1, seed_gamma, 0.0) * scale
        d0[pl.ds(at, count)] = diagonal[:, 0:8] * (1.0 / damping)
        for slot, value in enumerate((px[1:], py, my, pz, mass)):
            fine[slot, pl.ds(at, count)] = value[:, 0:8]
        return carry

    lax.fori_loop(0, 30 // count, fine_turn, 0, unroll=True)

    op1 = coarsen(
        (fine[0, 3:28], fine[1, 4:28], fine[2, 4:28], fine[3, 4:28], fine[4, 4:28]), 1
    )
    px, py, _, pz, mass = op1
    ybit, zbit = odd(py, 1, 1), odd(py, 1, 2)
    p1[6:18, 0:8, :] = jnp.where(ybit, jnp.where(zbit, mass, pz), jnp.where(zbit, py, px[1:]))
    scale1 = damping / own_diagonal(op1, 2)
    s1[...] = scale1

    def send_1(ref, which, near, whole, corners):
        for dx, dy in MIDDLE:
            if abs(dy) == 2:
                parts = [(*{1: (4, 20), -1: (0, 16)}[dy // 2], 4, corners[2])]
            elif dx and dy:
                close, far = {1: ((4, 28), (0, 24)), -1: ((0, 8), (4, 12))}[dy]
                parts = [(*close, 4, corners[0]), (*far, 4, corners[1])]
            else:
                parts = [(0, {0: 0, 1: 24, -1: 8}[dy], 8, near)]
            for sy, ty, ny, n in parts:
                nx = n if dx else whole
                sx = near + (whole - n if dx == 1 else 0)
                tx = {1: near - n, -1: near + whole, 0: near}[dx]
                send(
                    ref.at[sx : sx + nx, sy : sy + ny], ref.at[tx : tx + nx, ty : ty + ny],
                    which, device(dx, dy),
                )

    send_1(p1, 2, 6, 12, (5, 3, 1))
    groups[2] = p1.at[0:24, 0:22]

    sweep(b0, va0, 2, 29, 4, w0, b0, 1, 1)

    def residual_0(index, carry):
        at = 4 + 6 * index
        here, total = step(va0, at, 6, w0, b0, 1, 1, 8)
        r = pair_x(d0[pl.ds(at, 6)] * (total - here))
        r = pair(pair(r, 1, 1), 1, 2) * s1[pl.ds(3 * index, 3)]
        ybit, zbit = odd(r[0:1], 1, 1), odd(r[0:1], 1, 2)
        b1p[pl.ds(2 + index, 1), 0:8, :] = jnp.where(zbit, jnp.where(ybit, r[2:3], r[1:2]), r[0:1])
        return carry

    lax.fori_loop(0, 4, residual_0, 0, unroll=True)
    send_1(b1p, 3, 2, 4, (2, 1, 1))
    groups[3] = b1p.at[0:6]

    op2 = coarsen(op1, 2)
    px, py, _, pz, mass = op2
    slot = place(py.shape, 2) % 4
    packed = jnp.where(slot == 0, px[1:], jnp.where(slot == 1, py, jnp.where(slot == 2, pz, mass)))
    p2[6:12, 0:2, :] = jnp.where(place(packed.shape, 1) == 0, packed, up(packed, 3, 1))[:, 0:2]

    def send_2(ref, which):
        for dx, dy in MIDDLE:
            n = 6 if dx == 0 else 2 if abs(dy) == 2 else 4
            sx = 12 - n if dx == 1 else 6
            tx = {1: 6 - n, -1: 12, 0: 6}[dx]
            ty = -2 * dy % 16
            send(ref.at[sx : sx + n, 0:2], ref.at[tx : tx + n, ty : ty + 2], which, device(dx, dy))
        groups[which] = ref.at[0:7]

    send_2(p2, 4)

    op3 = coarsen(op2, 4)
    s3 = damping / own_diagonal(op3, 8)
    px, py, _, pz, mass = op3
    for index, value in enumerate((px[1:], py, pz, mass)):
        o3[3 * index : 3 * index + 3] = value

    def gather_plane(source, target, which):
        seat = core * 8 + chip_y
        target[:, pl.ds(seat, 1), :] = source[:, 0:1, :]
        each(16, lambda k: send(source.at[:, 0:1], target.at[:, pl.ds(seat, 1)], which, in_plane(k)))
        groups[which] = target.at[:, 0:15]

    def merge(source, target, kinds):
        rows = source[...]
        rows = jnp.where(place(rows.shape, 2) % 8 == place(rows.shape, 1) % 8, rows, 0.0)
        rows = rows.reshape(3 * kinds * 2, 8, BZ)
        for distance in (1, 2, 4):
            rows = rows + up(rows, distance, 1)
        target[...] = rows.reshape(kinds, 3, 2, 8, BZ)

    def gather_column(source, target, which, kinds):
        piece = source.at[kinds, :, :, 0:1]
        seat = target.at[kinds, half, :, pl.ds(gy % 4 // 2 * 2, 2), pl.ds(gy // 4, 1)]
        pltpu.make_async_copy(piece, seat, recv_sem.at[which]).start()
        each(32, lambda k: send(piece, seat, which, in_column(k)))

    gather_plane(o3, g1o, 6)

    arrived(2)

    def weights_1(index, carry):
        at = 1 + 2 * index
        packed = p1[pl.ds(at - 1, 3)]
        even_z, odd_z = low(packed, 1, 2), high(packed[1:], 1, 2)
        px, pz = low(even_z, 1, 1), high(even_z[1:], 1, 1)
        py, mass = low(odd_z, 1, 1), high(odd_z, 1, 1)
        diagonal, _ = normalise(px[1:], px[:-1], py, down(py, 2, 1), pz, down(pz, 2, 2), mass, w1, at, 2)
        d1[pl.ds(at, 2)] = diagonal * (1.0 / damping)
        return carry

    lax.fori_loop(0, 11, weights_1, 0, unroll=True)
    arrived(3)

    def unpack_1(index, carry):
        packed = b1p[pl.ds(index, 1)]
        odd_z = high(packed, 1, 2)
        b1[pl.ds(3 * index, 1)] = low(packed, 1, 2)
        b1[pl.ds(3 * index + 1, 1)] = low(odd_z, 1, 1)
        b1[pl.ds(3 * index + 2, 1)] = high(odd_z, 1, 1)
        return carry

    lax.fori_loop(0, 8, unpack_1, 0, unroll=True)
    sweep(b1, va1, 1, 22, 2, w1, b1, 2, 2)

    arrived(4)

    def weights_2(index, carry):
        at = 1 + 4 * index
        packed = p2[pl.ds(at - 1, 5)]
        even_z, odd_z = low(packed, 1, 2), high(packed[1:], 1, 2)
        px, pz = low(even_z, 2, 2), high(even_z[1:], 2, 2)
        py, mass = low(odd_z, 2, 2), high(odd_z, 2, 2)
        diagonal, scale = normalise(px[1:], px[:-1], py, down(py, 1, 1), pz, down(pz, 4, 2), mass, w2, at, 4)
        d2[pl.ds(at, 4)] = diagonal * (1.0 / damping)
        s2[pl.ds(at, 4)] = scale
        return carry

    lax.fori_loop(0, 4, weights_2, 0, unroll=True)

    def residual_1(index, carry):
        at = 2 + 4 * index
        here, total = step(va1, at, 4, w1, b1, 2, 2)
        r = pair_x(d1[pl.ds(at, 4)] * (total - here))
        r = pair(pair(r, 2, 1), 2, 2)
        mine, after, before = r[:, 0:8], r[:, 8:16], r[:, 24:32]
        row = place(mine.shape, 1)
        first = jnp.where(row < 2, jnp.where(row == 0, mine, up(mine, 3, 1)), jnp.where(row == 2, down(after, 2, 1), up(after, 1, 1)))
        last = jnp.where(row == 7, down(before, 3, 1), up(before, 2, 1))
        to = pl.ds(4 + 2 * index, 2)
        b2[to, 0:8, :] = first * s2[to, 0:8, :]
        b2[to, 8:16, :] = last * s2[to, 8:16, :]
        return carry

    lax.fori_loop(0, 5, residual_1, 0, unroll=True)

    sweep(b2, va2, 5, 12, 4, w2, b2, 1, 4)
    here, total = step(va2, 6, 6, w2, b2, 1, 4, 8)
    r = pair_x(d2[6:12, 0:8, :] * (total - here))
    r = pair(pair(r, 1, 1), 4, 2)
    o4[...] = r * s3
    gather_plane(o4, g1, 8)

    arrived(6)
    merge(g1o, qo, 4)
    half_kinds = pl.ds(2 * core, 2)
    gather_column(qo, g2o, 7, half_kinds)
    groups[7] = g2o.at[0:2]
    zbit = odd(here[:, 0:2], 1, 2)
    x2[6:12, 0:2, :] = jnp.where(zbit, b2[6:12, 0:2, :], here[:, 0:2])
    send_2(x2, 5)

    arrived(8)
    merge(g1, q, 1)
    gather_column(q, g2, 9, pl.ds(0, 1))
    groups[9] = g2

    arrived(7)
    send(g2o.at[half_kinds], g2o.at[half_kinds], 10, (gx, gy + 1 - 2 * core))
    groups[10] = g2o.at[0:2]
    arrived(5)
    b2[...] = high(x2[...], 1, 2)
    va2[...] = low(x2[...], 1, 2)

    whole = (3, 4, 2, 8, BZ)

    def lanes(v, shift):
        return pltpu.roll(v.reshape(-1, 8, BZ), shift, 2).reshape(v.shape)

    def rows(v, shift):
        return pltpu.roll(v.reshape(-1, 8, BZ), shift, 1).reshape(v.shape)

    def spread(v):
        second = odd(v[0], 8, 3)
        return jnp.stack(
            [jnp.where(second, lanes(v[1], 8), v[0]), jnp.where(second, v[1], lanes(v[0], BZ - 8))],
            axis=2,
        )

    def around(v):
        return (
            jnp.concatenate([v[1:], lanes(v[:1], BZ - 1)], axis=0),
            jnp.concatenate([lanes(v[2:], 1), v[:2]], axis=0),
            jnp.concatenate([v[:, 1:], rows(v[:, :1], 7)], axis=1),
            jnp.concatenate([rows(v[:, 3:], 1), v[:, :3]], axis=1),
            jnp.concatenate([v[:, :, 1:], lanes(v[:, :, :1], BZ - 16)], axis=2),
            jnp.concatenate([lanes(v[:, :, 1:], 16), v[:, :, :1]], axis=2),
        )

    arrived(10)
    px, py, pz, mass = [spread(g2o[k]) for k in range(4)]
    mx, my, mz = around(px)[1], around(py)[3], around(pz)[5]
    scale = damping / (mass + px + mx + py + my + pz + mz)
    for index, value in enumerate((px, mx, py, my, pz, mz)):
        w3[index] = value * scale
    arrived(9)
    b3[...] = spread(g2[0])

    def solve(index, v):
        total = (1.0 - damping) * v + b3[...]
        for k, n in enumerate(around(v)):
            total = total + w3[k] * n
        return total

    solved[...] = lax.fori_loop(1, COARSE_ITERS, solve, b3[...], unroll=True)

    row = (place((16, BZ), 0) // 2 + 2) % 8
    slot = place((16, BZ), 1) % 16
    for j in range(-2, 5):
        at = (3 * gx + j + 48) % 48
        tiles = []
        for z_low in range(2):
            tile = jnp.zeros((16, BZ), f32)
            for k in range(-2, 3):
                y = (gy + k + GY) % GY
                line = solved[pl.ds(at % 3, 1), pl.ds(y % 4, 1), z_low, pl.ds(y // 4, 1), :]
                tile = jnp.where(row == k + 2, line.reshape(1, BZ), tile)
            tiles.append(pair(jnp.where(slot == at // 3, tile, 0.0), 8, 1))
        tile = jnp.where(slot >= 8, tiles[1], tiles[0])
        tile = pair(pair(pair(tile, 1, 1), 2, 1), 4, 1)
        va2[6 + 2 * j : 8 + 2 * j] = va2[6 + 2 * j : 8 + 2 * j] + tile[None]
    sweep(va2, vb2, 3, 14, 4, w2, b2, 1, 4)
    sweep(vb2, va2, 4, 13, 5, w2, b2, 1, 4)

    upper = place((1, 8, BZ), 1) >= 4

    def correct_1(index, carry):
        for rows, first in ((0, 0), (8, 2), (24, 14)):
            a = va2[pl.ds(4 + index, 1), first : first + 1, :]
            b = va2[pl.ds(4 + index, 1), first + 1 : first + 2, :]
            at = pl.ds(2 + 2 * index, 2)
            va1[at, rows : rows + 8, :] = va1[at, rows : rows + 8, :] + jnp.where(upper, b, a)
        return carry

    lax.fori_loop(0, 10, correct_1, 0, unroll=True)
    sweep(va1, vb1, 4, 19, 2, w1, b1, 2, 2)
    sweep(vb1, va1, 5, 18, 2, w1, b1, 2, 2)

    def correct_0(index, carry):
        at = pl.ds(2 + 2 * index, 2)
        coarse = va1[pl.ds(5 + index, 1)]
        va0[at, 0:8, :] = va0[at, 0:8, :] + coarse[:, 0:8]
        va0[at, 8:16, :] = va0[at, 8:16, :] + jnp.where(upper, coarse[:, 24:32], coarse[:, 8:16])
        return carry

    lax.fori_loop(0, 14, correct_0, 0, unroll=True)
    sweep(va0, vb0, 2, 29, 4, w0, b0, 1, 1)

    def finish(index, carry):
        at = 4 + 4 * index
        _, total = step(vb0, at, 4, w0, b0, 1, 1, 8)
        out[pl.ds(4 * index, 4)] = total
        return carry

    lax.fori_loop(0, 6, finish, 0, unroll=True)

    for which in (0, 1, 2, 3, 4, 5, 6, 8, 10):
        await_bytes(groups[which], send_sem.at[which])
    await_bytes(p1.at[0:12, 0:31], send_sem.at[7])
    await_bytes(p1.at[0:6, 0:31], send_sem.at[9])


def shards(intensities, labels):
    def vmem(*shape, dtype=f32):
        return pltpu.VMEM(shape, dtype)

    zero, one, two = (32, 16, BZ), (24, 32, BZ), (18, 16, BZ)
    return pl.pallas_call(
        kernel,
        out_shape=jax.ShapeDtypeStruct((BX, BY, BZ), f32),
        in_specs=[pl.BlockSpec(memory_space=pltpu.HBM)] * 2,
        out_specs=pl.BlockSpec(memory_space=pltpu.VMEM),
        scratch_shapes=[
            vmem(*zero, dtype=jnp.int32), vmem(*zero, dtype=jnp.int32),
            [vmem(*zero)] * 6, vmem(*zero), vmem(32, 8, BZ), vmem(5, 32, 8, BZ),
            vmem(*zero), vmem(*zero),
            vmem(*one), vmem(8, 32, BZ), vmem(*one), [vmem(*one)] * 6, vmem(*one), vmem(12, 8, BZ),
            vmem(*one), vmem(*one),
            vmem(*two), vmem(*two), vmem(*two), [vmem(*two)] * 6, vmem(*two), vmem(*two),
            vmem(*two), vmem(*two),
            vmem(12, 8, BZ), vmem(12, 16, BZ), vmem(4, 3, 2, 8, BZ), vmem(4, 2, 3, 4, 8, BZ),
            vmem(3, 8, BZ), vmem(3, 16, BZ), vmem(1, 3, 2, 8, BZ), vmem(1, 2, 3, 4, 8, BZ),
            vmem(6, 3, 4, 2, 8, BZ), vmem(3, 4, 2, 8, BZ), vmem(3, 4, 2, 8, BZ),
            pltpu.SemaphoreType.DMA((2,)),
            pltpu.SemaphoreType.DMA((11,)),
            pltpu.SemaphoreType.DMA((11,)),
        ],
        compiler_params=pltpu.CompilerParams(
            collective_id=0, has_side_effects=True, vmem_limit_bytes=40 * 1024 * 1024
        ),
        name="v_cycle",
    )(intensities, labels)


def solution(mesh):
    return jax.shard_map(
        shards,
        mesh=mesh,
        in_specs=(P("gx", "gy", None), P("gx", "gy", None)),
        out_specs=P("gx", "gy", None),
        check_vma=False,
    )
```

```python
import jax
import jax.numpy as jnp
from jax import lax
from jax.experimental import pallas as pl
from jax.experimental.pallas import tpu as pltpu
from jax.sharding import PartitionSpec as P

COARSE_ITERS = 30

edge_beta = 3.0
seed_gamma = 4.0
base_mass = 0.1
damping = 0.7

MESH = pl.DeviceIdType.MESH
f32 = jnp.float32

BX, BY, BZ = 24, 8, 128
GX, GY = 16, 32

NEAR = [(dx, dy) for dx in (-1, 0, 1) for dy in (-1, 0, 1) if (dx, dy) != (0, 0)]
MIDDLE = [(dx, dy) for dx in (-1, 1, 0) for dy in (0, -1, 1, -2, 2) if (dx, dy) != (0, 0)]


def place(shape, axis):
    return lax.broadcasted_iota(jnp.int32, shape, axis)


def up(array, distance, axis):
    return pltpu.roll(array, array.shape[axis] - distance, axis)


def down(array, distance, axis):
    return pltpu.roll(array, distance, axis)


def odd(array, distance, axis):
    return (place(array.shape, axis) // distance) % 2 == 1


def high(array, distance, axis):
    return jnp.where(odd(array, distance, axis), array, up(array, distance, axis))


def low(array, distance, axis):
    return jnp.where(odd(array, distance, axis), down(array, distance, axis), array)


def pair(array, distance, axis):
    return array + jnp.where(
        odd(array, distance, axis), down(array, distance, axis), up(array, distance, axis)
    )


def halves(array):
    split = array.reshape((array.shape[0] // 2, 2) + array.shape[1:])
    return split[:, 0], split[:, 1]


def pair_x(array):
    first, second = halves(array)
    return first + second


def coarsen(operator, distance):
    px, py, my, pz, mass = operator
    next_px = jnp.concatenate([px[0:1], halves(px[1:])[1]], axis=0)
    next_px = pair(pair(next_px, distance, 1), distance, 2)
    next_py = high(pair(pair_x(py), distance, 2), distance, 1)
    next_my = low(pair(pair_x(my), distance, 2), distance, 1)
    next_pz = high(pair(pair_x(pz), distance, 1), distance, 2)
    next_mass = pair(pair(pair_x(mass), distance, 1), distance, 2)
    return next_px, next_py, next_my, next_pz, next_mass


def own_diagonal(operator, distance):
    px, py, my, pz, mass = operator
    return mass + px[1:] + px[:-1] + py + my + pz + down(pz, distance, 2)


def weight(upper, lower):
    gap = upper - lower
    return jnp.exp(gap * gap * (-edge_beta / (255.0 * 255.0)))


def step(source, first, count, weights, rhs, dist_y, dist_z, rows=None):
    v = source[pl.ds(first - 1, count + 2)]
    c = v[1:-1]
    near = [v[2:], v[:-2], up(c, dist_y, 1), down(c, dist_y, 1), up(c, dist_z, 2), down(c, dist_z, 2)]
    rows = c.shape[1] if rows is None else rows
    here = c[:, :rows]
    total = (1.0 - damping) * here + rhs[pl.ds(first, count), 0:rows, :]
    for w, n in zip(weights, near):
        total = total + w[pl.ds(first, count), 0:rows, :] * n[:, :rows]
    return here, total


def sweep(source, target, first, last, count, weights, rhs, dist_y, dist_z):
    def turn(index, carry):
        at = first + index * count
        _, total = step(source, at, count, weights, rhs, dist_y, dist_z)
        target[pl.ds(at, count)] = total
        return carry

    lax.fori_loop(0, (last + 1 - first) // count, turn, 0, unroll=True)


def normalise(px, px_before, py, my, pz, mz, mass, stores, at, count):
    diagonal = mass + px + px_before + py + my + pz + mz
    scale = damping / diagonal
    for store, value in zip(stores, (px, px_before, py, my, pz, mz)):
        store[pl.ds(at, count)] = value * scale
    return diagonal, scale


def kernel(
    ints, labels, out,
    ibuf, lbuf, obuf, w0, b0, d0, fine, va0, vb0,
    p1, b1p, b1, w1, d1, s1, va1, vb1,
    p2, x2, b2, w2, d2, s2, va2, vb2,
    o3, g1o, qo, g2o, o4, g1, q, g2, w3, b3, solved,
    local_sem, send_sem, recv_sem,
):
    gx, gy = lax.axis_index("gx"), lax.axis_index("gy")
    half, chip_y = gx // 8, gx % 8
    chip_z, chip_x, core = half * 4 + gy // 8, gy % 8 // 2, gy % 2
    groups = {}

    def device(dx, dy):
        return (lax.rem(gx + dx + GX, GX), lax.rem(gy + dy + GY, GY))

    def offset(k, size):
        return (size // 2 + (k + 1) // 2 * (1 - 2 * (k % 2))) % size

    def in_plane(k):
        return (half * 8 + (chip_y + offset(k // 2, 8)) % 8, gy - core + (core + k + 1) % 2)

    def in_column(k):
        z = (chip_z + offset(k // 4, 8)) % 8
        x = (chip_x + offset(k % 4, 4)) % 4
        return (z // 4 * 8 + chip_y, z % 4 * 8 + x * 2 + core)

    def send(source, target, which, to):
        pltpu.make_async_remote_copy(
            source, target, send_sem.at[which], recv_sem.at[which],
            device_id=to, device_id_type=MESH,
        ).start()

    def each(count, action):
        def turn(index, carry):
            action(index)
            return carry

        lax.fori_loop(0, count, turn, 0)

    def await_bytes(ref, sem):
        pltpu.make_async_copy(ref, ref, sem).wait()

    def arrived(which):
        await_bytes(groups[which], recv_sem.at[which])

    own = [
        pltpu.make_async_copy(ints, ibuf.at[4:28, 0:8], local_sem.at[0]),
        pltpu.make_async_copy(labels, lbuf.at[4:28, 0:8], local_sem.at[1]),
    ]
    for copy in own:
        copy.start()
    barrier = pltpu.get_barrier_semaphore()

    def greet(to):
        pl.semaphore_signal(barrier, inc=1, device_id=to, device_id_type=MESH)

    for dx, dy in MIDDLE:
        greet(device(dx, dy))
    each(31, lambda k: greet(in_column(k)))
    each(15, lambda k: greet(in_plane(k)))
    p2[:, 6:12, :] = jnp.ones((18, 6, BZ), f32)
    x2[:, 6:12, :] = jnp.zeros((18, 6, BZ), f32)
    pl.semaphore_wait(barrier, len(MIDDLE) + 15 + 31)

    for copy in own:
        copy.wait()

    def send_inputs(target, which, pairs, depth, corner_x, corner_y):
        for dx, dy in pairs:
            n, m = (corner_x, corner_y) if dx and dy else (depth, depth)
            sx, tx = {1: (28 - n, 4 - n), -1: (4, 28), 0: (4, 4)}[dx]
            sy, ty = {1: (8 - m, 16 - m), -1: (0, 8), 0: (0, 0)}[dy]
            nx, ny = n if dx else 24, m if dy else 8
            send(
                target.at[sx : sx + nx, sy : sy + ny], target.at[tx : tx + nx, ty : ty + ny],
                which, device(dx, dy),
            )

    aside = [d for d in NEAR if d[0] == 0]
    ahead = [(1, 0), (-1, 0), (1, 1), (1, -1), (-1, 1), (-1, -1)]
    send_inputs(ibuf, 11, ahead, 4, 3, 4)
    send_inputs(lbuf, 12, ahead, 3, 2, 2)
    send_inputs(ibuf, 0, aside, 4, 3, 4)
    send_inputs(lbuf, 1, aside, 3, 2, 2)
    groups[0], groups[1] = ibuf.at[0:12], lbuf.at[0:9]
    groups[11], groups[12] = ibuf.at[0:7], lbuf.at[0:4]
    arrived(0)
    arrived(1)

    def fine_operator(at, count):
        wide = ibuf[pl.ds(at - 1, count + 2)].astype(f32)
        lab = lbuf[pl.ds(at, count)]
        c = wide[1:-1]
        px = weight(wide[1:], wide[:-1])
        gone_x = gx * BX + (at - 5) + place(px.shape, 0)
        px = jnp.where((gone_x == GX * BX - 1) | (gone_x == -1), 0.0, px)
        row = place(c.shape, 1)
        gone_y = gy * BY + jnp.where(row >= 12, row - 16, row)
        py = jnp.where((gone_y == GY * BY - 1) | (gone_y == -1), 0.0, weight(up(c, 1, 1), c))
        my = down(py, 1, 1)
        pz = jnp.where(place(c.shape, 2) == BZ - 1, 0.0, weight(up(c, 1, 2), c))
        mz = down(pz, 1, 2)
        mass = base_mass + jnp.where(lab > 0, seed_gamma, 0.0)
        diagonal, scale = normalise(px[1:], px[:-1], py, my, pz, mz, mass, w0, at, count)
        b0[pl.ds(at, count)] = jnp.where(lab == 1, seed_gamma, 0.0) * scale
        d0[pl.ds(at, count)] = diagonal[:, 0:8] * (1.0 / damping)
        for slot, value in enumerate((px[1:], py, my, pz, mass)):
            fine[slot, pl.ds(at, count)] = value[:, 0:8]

    def level_1(first, last):
        at, end = 4 + 2 * first, 6 + 2 * last
        return coarsen((fine[0, at - 1 : end], *(fine[slot, at:end] for slot in range(1, 5))), 1)

    def packed_1(operator):
        px, py, _, pz, mass = operator
        ybit, zbit = odd(py, 1, 1), odd(py, 1, 2)
        return jnp.where(ybit, jnp.where(zbit, mass, pz), jnp.where(zbit, py, px[1:]))

    def send_1(ref, which, near, whole, corners, ends):
        for dx, dy in MIDDLE:
            if abs(dy) == 2:
                parts = [(*{1: (4, 20), -1: (0, 16)}[dy // 2], 4, corners[2])]
            elif dx and dy and corners[0] == corners[1]:
                parts = [(0, {1: 24, -1: 8}[dy], 8, corners[0])]
            elif dx and dy:
                close, far = {1: ((4, 28), (0, 24)), -1: ((0, 8), (4, 12))}[dy]
                parts = [(*close, 4, corners[0]), (*far, 4, corners[1])]
            else:
                parts = [(0, {0: 0, 1: 24, -1: 8}[dy], 8, near)]
            for sy, ty, ny, n in parts:
                nx = n - ends if dx else whole - 2 * ends
                sx = near + {1: whole - n, -1: ends, 0: ends}[dx]
                tx = {1: near - n, -1: near + whole + ends, 0: near + ends}[dx]
                if nx > 0:
                    send(
                        ref.at[sx : sx + nx, sy : sy + ny], ref.at[tx : tx + nx, ty : ty + ny],
                        which, device(dx, dy),
                    )

    for at in (5, 16):
        fine_operator(at, 11)
    inner = level_1(1, 10)
    p1[7:17, 0:8, :] = packed_1(inner)
    send_1(p1, 2, 6, 12, (5, 3, 1), 1)
    groups[2] = p1.at[0:13]
    sweep(b0, va0, 6, 25, 4, w0, b0, 1, 1)
    arrived(11)
    arrived(12)
    fine_operator(1, 4)
    fine_operator(27, 4)

    lower, upper = level_1(0, 0), level_1(11, 11)
    b1p[3:4, 0:8, :] = packed_1(lower)
    b1p[8:9, 0:8, :] = packed_1(upper)
    op1 = (
        jnp.concatenate([lower[0][0:1], inner[0], upper[0][1:2]], axis=0),
        *(jnp.concatenate(parts, axis=0) for parts in zip(lower[1:], inner[1:], upper[1:])),
    )
    s1[...] = damping / own_diagonal(op1, 2)

    sweep(b0, va0, 2, 5, 4, w0, b0, 1, 1)
    sweep(b0, va0, 26, 29, 4, w0, b0, 1, 1)

    def residual_0(index, carry):
        at = 4 + 6 * index
        here, total = step(va0, at, 6, w0, b0, 1, 1, 8)
        r = pair_x(d0[pl.ds(at, 6)] * (total - here))
        r = pair(pair(r, 1, 1), 1, 2) * s1[pl.ds(3 * index, 3)]
        ybit, zbit = odd(r[0:1], 1, 1), odd(r[0:1], 1, 2)
        b1p[pl.ds(4 + index, 1), 0:8, :] = jnp.where(zbit, jnp.where(ybit, r[2:3], r[1:2]), r[0:1])
        return carry

    lax.fori_loop(0, 4, residual_0, 0, unroll=True)
    send_1(b1p, 3, 3, 6, (3, 3, 2), 0)
    groups[3] = b1p.at[0:10]

    op2 = coarsen(op1, 2)
    px, py, _, pz, mass = op2
    slot = place(py.shape, 2) % 4
    packed = jnp.where(slot == 0, px[1:], jnp.where(slot == 1, py, jnp.where(slot == 2, pz, mass)))
    p2[6:12, 0:2, :] = jnp.where(place(packed.shape, 1) == 0, packed, up(packed, 3, 1))[:, 0:2]

    def send_2(ref, which):
        for dx, dy in MIDDLE:
            n = 6 if dx == 0 else 2 if abs(dy) == 2 else 4
            sx = 12 - n if dx == 1 else 6
            tx = {1: 6 - n, -1: 12, 0: 6}[dx]
            ty = -2 * dy % 16
            send(ref.at[sx : sx + n, 0:2], ref.at[tx : tx + n, ty : ty + 2], which, device(dx, dy))
        groups[which] = ref.at[0:7]

    send_2(p2, 4)

    op3 = coarsen(op2, 4)
    s3 = damping / own_diagonal(op3, 8)
    px, py, _, pz, mass = op3
    for index, value in enumerate((px[1:], py, pz, mass)):
        o3[3 * index : 3 * index + 3] = value

    def gather_plane(source, target, which):
        seat = core * 8 + chip_y
        target[:, pl.ds(seat, 1), :] = source[:, 0:1, :]
        each(15, lambda k: send(source.at[:, 0:1], target.at[:, pl.ds(seat, 1)], which, in_plane(k)))
        groups[which] = target.at[:, 0:15]

    def merge(source, target, kinds):
        rows = source[...]
        rows = jnp.where(place(rows.shape, 2) % 8 == place(rows.shape, 1) % 8, rows, 0.0)
        rows = rows.reshape(3 * kinds * 2, 8, BZ)
        for distance in (1, 2, 4):
            rows = rows + up(rows, distance, 1)
        target[...] = rows.reshape(kinds, 3, 2, 8, BZ)

    def gather_column(source, target, which, kinds):
        piece = source.at[kinds, :, :, 0:1]
        seat = target.at[kinds, half, :, pl.ds(gy % 4 // 2 * 2, 2), pl.ds(gy // 4, 1)]
        pltpu.make_async_copy(piece, seat, recv_sem.at[which]).start()
        each(31, lambda k: send(piece, seat, which, in_column(k)))

    gather_plane(o3, g1o, 6)

    arrived(2)

    def weights_1(at, count):
        packed = p1[at - 1 : at + count]
        even_z, odd_z = low(packed, 1, 2), high(packed[1:], 1, 2)
        px, pz = low(even_z, 1, 1), high(even_z[1:], 1, 1)
        py, mass = low(odd_z, 1, 1), high(odd_z, 1, 1)
        diagonal, _ = normalise(px[1:], px[:-1], py, down(py, 2, 1), pz, down(pz, 2, 2), mass, w1, at, count)
        d1[at : at + count] = diagonal * (1.0 / damping)

    for at, count in ((1, 4), (8, 3), (11, 3), (14, 3), (20, 3)):
        weights_1(at, count)
    arrived(3)
    for plane, end in ((5, 2), (6, 3), (17, 8), (18, 9)):
        p1[plane] = b1p[end]
    for at in (5, 17):
        weights_1(at, 3)
    for index, plane in enumerate((0, 1, 4, 5, 6, 7, 10, 11)):
        packed = b1p[plane : plane + 1]
        odd_z = high(packed, 1, 2)
        b1[3 * index : 3 * index + 1] = low(packed, 1, 2)
        b1[3 * index + 1 : 3 * index + 2] = low(odd_z, 1, 1)
        b1[3 * index + 2 : 3 * index + 3] = high(odd_z, 1, 1)
    sweep(b1, va1, 1, 22, 2, w1, b1, 2, 2)

    arrived(4)

    def weights_2(index, carry):
        at = 1 + 4 * index
        packed = p2[pl.ds(at - 1, 5)]
        even_z, odd_z = low(packed, 1, 2), high(packed[1:], 1, 2)
        px, pz = low(even_z, 2, 2), high(even_z[1:], 2, 2)
        py, mass = low(odd_z, 2, 2), high(odd_z, 2, 2)
        diagonal, scale = normalise(px[1:], px[:-1], py, down(py, 1, 1), pz, down(pz, 4, 2), mass, w2, at, 4)
        d2[pl.ds(at, 4)] = diagonal * (1.0 / damping)
        s2[pl.ds(at, 4)] = scale
        return carry

    lax.fori_loop(0, 4, weights_2, 0, unroll=True)

    def residual_1(index, carry):
        at = 2 + 4 * index
        here, total = step(va1, at, 4, w1, b1, 2, 2)
        r = pair_x(d1[pl.ds(at, 4)] * (total - here))
        r = pair(pair(r, 2, 1), 2, 2)
        mine, after, before = r[:, 0:8], r[:, 8:16], r[:, 24:32]
        row = place(mine.shape, 1)
        first = jnp.where(row < 2, jnp.where(row == 0, mine, up(mine, 3, 1)), jnp.where(row == 2, down(after, 2, 1), up(after, 1, 1)))
        last = jnp.where(row == 7, down(before, 3, 1), up(before, 2, 1))
        to = pl.ds(4 + 2 * index, 2)
        b2[to, 0:8, :] = first * s2[to, 0:8, :]
        b2[to, 8:16, :] = last * s2[to, 8:16, :]
        return carry

    lax.fori_loop(0, 5, residual_1, 0, unroll=True)

    sweep(b2, va2, 5, 12, 4, w2, b2, 1, 4)
    here, total = step(va2, 6, 6, w2, b2, 1, 4, 8)
    r = pair_x(d2[6:12, 0:8, :] * (total - here))
    r = pair(pair(r, 1, 1), 4, 2)
    o4[...] = r * s3
    gather_plane(o4, g1, 8)

    arrived(6)
    merge(g1o, qo, 4)
    half_kinds = pl.ds(2 * core, 2)
    gather_column(qo, g2o, 7, half_kinds)
    groups[7] = g2o.at[0:2]
    zbit = odd(here[:, 0:2], 1, 2)
    x2[6:12, 0:2, :] = jnp.where(zbit, b2[6:12, 0:2, :], here[:, 0:2])
    send_2(x2, 5)

    arrived(8)
    merge(g1, q, 1)
    gather_column(q, g2, 9, pl.ds(0, 1))
    groups[9] = g2

    arrived(7)
    send(g2o.at[half_kinds], g2o.at[half_kinds], 10, (gx, gy + 1 - 2 * core))
    groups[10] = g2o.at[0:2]
    arrived(5)
    b2[...] = high(x2[...], 1, 2)
    va2[...] = low(x2[...], 1, 2)

    whole = (3, 4, 2, 8, BZ)

    def lanes(v, shift):
        return pltpu.roll(v.reshape(-1, 8, BZ), shift, 2).reshape(v.shape)

    def rows(v, shift):
        return pltpu.roll(v.reshape(-1, 8, BZ), shift, 1).reshape(v.shape)

    def spread(v):
        second = odd(v[0], 8, 3)
        return jnp.stack(
            [jnp.where(second, lanes(v[1], 8), v[0]), jnp.where(second, v[1], lanes(v[0], BZ - 8))],
            axis=2,
        )

    def around(v):
        return (
            jnp.concatenate([v[1:], lanes(v[:1], BZ - 1)], axis=0),
            jnp.concatenate([lanes(v[2:], 1), v[:2]], axis=0),
            jnp.concatenate([v[:, 1:], rows(v[:, :1], 7)], axis=1),
            jnp.concatenate([rows(v[:, 3:], 1), v[:, :3]], axis=1),
            jnp.concatenate([v[:, :, 1:], lanes(v[:, :, :1], BZ - 16)], axis=2),
            jnp.concatenate([lanes(v[:, :, 1:], 16), v[:, :, :1]], axis=2),
        )

    arrived(10)
    px, py, pz, mass = [spread(g2o[k]) for k in range(4)]
    mx, my, mz = around(px)[1], around(py)[3], around(pz)[5]
    scale = damping / (mass + px + mx + py + my + pz + mz)
    for index, value in enumerate((px, mx, py, my, pz, mz)):
        w3[index] = value * scale
    arrived(9)
    b3[...] = spread(g2[0])

    def solve(index, v):
        total = (1.0 - damping) * v + b3[...]
        for k, n in enumerate(around(v)):
            total = total + w3[k] * n
        return total

    solved[...] = lax.fori_loop(1, COARSE_ITERS, solve, b3[...], unroll=True)

    row = (place((16, BZ), 0) // 2 + 2) % 8
    slot = place((16, BZ), 1) % 16
    for j in range(-2, 5):
        at = (3 * gx + j + 48) % 48
        tiles = []
        for z_low in range(2):
            tile = jnp.zeros((16, BZ), f32)
            for k in range(-2, 3):
                y = (gy + k + GY) % GY
                line = solved[pl.ds(at % 3, 1), pl.ds(y % 4, 1), z_low, pl.ds(y // 4, 1), :]
                tile = jnp.where(row == k + 2, line.reshape(1, BZ), tile)
            tiles.append(pair(jnp.where(slot == at // 3, tile, 0.0), 8, 1))
        tile = jnp.where(slot >= 8, tiles[1], tiles[0])
        tile = pair(pair(pair(tile, 1, 1), 2, 1), 4, 1)
        va2[6 + 2 * j : 8 + 2 * j] = va2[6 + 2 * j : 8 + 2 * j] + tile[None]
    sweep(va2, vb2, 3, 14, 4, w2, b2, 1, 4)
    sweep(vb2, va2, 4, 13, 5, w2, b2, 1, 4)

    second = place((1, 8, BZ), 1) >= 4

    def correct_1(index, carry):
        for rows, first in ((0, 0), (8, 2), (24, 14)):
            a = va2[pl.ds(4 + index, 1), first : first + 1, :]
            b = va2[pl.ds(4 + index, 1), first + 1 : first + 2, :]
            at = pl.ds(2 + 2 * index, 2)
            va1[at, rows : rows + 8, :] = va1[at, rows : rows + 8, :] + jnp.where(second, b, a)
        return carry

    lax.fori_loop(0, 10, correct_1, 0, unroll=True)
    sweep(va1, vb1, 4, 19, 2, w1, b1, 2, 2)
    sweep(vb1, va1, 5, 18, 2, w1, b1, 2, 2)

    def correct_0(index, carry):
        at = pl.ds(2 + 2 * index, 2)
        coarse = va1[pl.ds(5 + index, 1)]
        va0[at, 0:8, :] = va0[at, 0:8, :] + coarse[:, 0:8]
        va0[at, 8:16, :] = va0[at, 8:16, :] + jnp.where(second, coarse[:, 24:32], coarse[:, 8:16])
        return carry

    lax.fori_loop(0, 14, correct_0, 0, unroll=True)
    sweep(va0, vb0, 2, 29, 4, w0, b0, 1, 1)

    results = []
    for at in (0, 8, 16):
        _, total = step(vb0, 4 + at, 8, w0, b0, 1, 1, 8)
        obuf[at : at + 8] = total
        results.append(pltpu.make_async_copy(obuf.at[at : at + 8], out.at[at : at + 8], local_sem.at[2 + at // 8]))
        results[-1].start()

    for which in (0, 1, 2, 3, 4, 5, 6, 8, 10, 11, 12):
        await_bytes(groups[which], send_sem.at[which])
    await_bytes(p1.at[0:12, 0:31], send_sem.at[7])
    await_bytes(p1.at[0:6, 0:31], send_sem.at[9])
    for copy in results:
        copy.wait()


def shards(intensities, labels):
    def vmem(*shape, dtype=f32):
        return pltpu.VMEM(shape, dtype)

    zero, one, two = (32, 16, BZ), (24, 32, BZ), (18, 16, BZ)
    return pl.pallas_call(
        kernel,
        out_shape=jax.ShapeDtypeStruct((BX, BY, BZ), f32),
        in_specs=[pl.BlockSpec(memory_space=pltpu.HBM)] * 2,
        out_specs=pl.BlockSpec(memory_space=pltpu.HBM),
        scratch_shapes=[
            vmem(*zero, dtype=jnp.int32), vmem(*zero, dtype=jnp.int32), vmem(BX, BY, BZ),
            [vmem(*zero)] * 6, vmem(*zero), vmem(32, 8, BZ), vmem(5, 32, 8, BZ),
            vmem(*zero), vmem(*zero),
            vmem(*one), vmem(12, 32, BZ), vmem(*one), [vmem(*one)] * 6, vmem(*one), vmem(12, 8, BZ),
            vmem(*one), vmem(*one),
            vmem(*two), vmem(*two), vmem(*two), [vmem(*two)] * 6, vmem(*two), vmem(*two),
            vmem(*two), vmem(*two),
            vmem(12, 8, BZ), vmem(12, 16, BZ), vmem(4, 3, 2, 8, BZ), vmem(4, 2, 3, 4, 8, BZ),
            vmem(3, 8, BZ), vmem(3, 16, BZ), vmem(1, 3, 2, 8, BZ), vmem(1, 2, 3, 4, 8, BZ),
            vmem(6, 3, 4, 2, 8, BZ), vmem(3, 4, 2, 8, BZ), vmem(3, 4, 2, 8, BZ),
            pltpu.SemaphoreType.DMA((5,)),
            pltpu.SemaphoreType.DMA((13,)),
            pltpu.SemaphoreType.DMA((13,)),
        ],
        compiler_params=pltpu.CompilerParams(
            collective_id=0, has_side_effects=True, vmem_limit_bytes=64 * 1024 * 1024
        ),
        name="v_cycle",
    )(intensities, labels)


def solution(mesh):
    return jax.shard_map(
        shards,
        mesh=mesh,
        in_specs=(P("gx", "gy", None), P("gx", "gy", None)),
        out_specs=P("gx", "gy", None),
        check_vma=False,
    )
```

```python
import jax
import jax.numpy as jnp
from jax import lax
from jax.experimental import pallas as pl
from jax.experimental.pallas import tpu as pltpu
from jax.sharding import PartitionSpec as P

COARSE_ITERS = 30

edge_beta = 3.0
seed_gamma = 4.0
base_mass = 0.1
damping = 0.7

MESH = pl.DeviceIdType.MESH
f32 = jnp.float32

BX, BY, BZ = 24, 8, 128
GX, GY = 16, 32

NEAR = [(dx, dy) for dx in (-1, 0, 1) for dy in (-1, 0, 1) if (dx, dy) != (0, 0)]
MIDDLE = [(dx, dy) for dx in (-1, 1, 0) for dy in (0, -1, 1, -2, 2) if (dx, dy) != (0, 0)]


def place(shape, axis):
    return lax.broadcasted_iota(jnp.int32, shape, axis)


def up(array, distance, axis):
    return pltpu.roll(array, array.shape[axis] - distance, axis)


def down(array, distance, axis):
    return pltpu.roll(array, distance, axis)


def odd(array, distance, axis):
    return (place(array.shape, axis) // distance) % 2 == 1


def high(array, distance, axis):
    return jnp.where(odd(array, distance, axis), array, up(array, distance, axis))


def low(array, distance, axis):
    return jnp.where(odd(array, distance, axis), down(array, distance, axis), array)


def pair(array, distance, axis):
    return array + jnp.where(
        odd(array, distance, axis), down(array, distance, axis), up(array, distance, axis)
    )


def halves(array):
    split = array.reshape((array.shape[0] // 2, 2) + array.shape[1:])
    return split[:, 0], split[:, 1]


def pair_x(array):
    first, second = halves(array)
    return first + second


def coarsen(operator, distance):
    px, py, my, pz, mass = operator
    next_px = jnp.concatenate([px[0:1], halves(px[1:])[1]], axis=0)
    next_px = pair(pair(next_px, distance, 1), distance, 2)
    next_py = high(pair(pair_x(py), distance, 2), distance, 1)
    next_my = low(pair(pair_x(my), distance, 2), distance, 1)
    next_pz = high(pair(pair_x(pz), distance, 1), distance, 2)
    next_mass = pair(pair(pair_x(mass), distance, 1), distance, 2)
    return next_px, next_py, next_my, next_pz, next_mass


def own_diagonal(operator, distance):
    px, py, my, pz, mass = operator
    return mass + px[1:] + px[:-1] + py + my + pz + down(pz, distance, 2)


def weight(upper, lower):
    gap = upper - lower
    return jnp.exp(gap * gap * (-edge_beta / (255.0 * 255.0)))


def step(source, first, count, weights, rhs, dist_y, dist_z, rows=None):
    v = source[pl.ds(first - 1, count + 2)]
    c = v[1:-1]
    near = [v[2:], v[:-2], up(c, dist_y, 1), down(c, dist_y, 1), up(c, dist_z, 2), down(c, dist_z, 2)]
    rows = c.shape[1] if rows is None else rows
    here = c[:, :rows]
    total = (1.0 - damping) * here + rhs[pl.ds(first, count), 0:rows, :]
    for w, n in zip(weights, near):
        total = total + w[pl.ds(first, count), 0:rows, :] * n[:, :rows]
    return here, total


def sweep(source, target, first, last, count, weights, rhs, dist_y, dist_z):
    def turn(index, carry):
        at = first + index * count
        _, total = step(source, at, count, weights, rhs, dist_y, dist_z)
        target[pl.ds(at, count)] = total
        return carry

    lax.fori_loop(0, (last + 1 - first) // count, turn, 0, unroll=True)


def normalise(px, px_before, py, my, pz, mz, mass, stores, at, count):
    diagonal = mass + px + px_before + py + my + pz + mz
    scale = damping / diagonal
    for store, value in zip(stores, (px, px_before, py, my, pz, mz)):
        store[pl.ds(at, count)] = value * scale
    return diagonal, scale


def kernel(
    ints, labels, out,
    ibuf, lbuf, w0, b0, d0, fine, va0, vb0,
    p1, b1p, b1, w1, d1, s1, va1, vb1,
    p2, x2, b2, w2, d2, s2, va2, vb2,
    o3, g1o, qo, g2o, o4, g1, q, g2, w3, b3, solved,
    local_sem, send_sem, recv_sem,
):
    gx, gy = lax.axis_index("gx"), lax.axis_index("gy")
    half, chip_y = gx // 8, gx % 8
    chip_z, chip_x, core = half * 4 + gy // 8, gy % 8 // 2, gy % 2
    groups = {}

    def device(dx, dy):
        return (lax.rem(gx + dx + GX, GX), lax.rem(gy + dy + GY, GY))

    def offset(k, size):
        return (size // 2 + (k + 1) // 2 * (1 - 2 * (k % 2))) % size

    def in_plane(k):
        return (half * 8 + (chip_y + offset(k // 2, 8)) % 8, gy - core + (core + k + 1) % 2)

    def in_column(k):
        z = (chip_z + offset(k // 4, 8)) % 8
        x = (chip_x + offset(k % 4, 4)) % 4
        return (z // 4 * 8 + chip_y, z % 4 * 8 + x * 2 + core)

    def send(source, target, which, to):
        pltpu.make_async_remote_copy(
            source, target, send_sem.at[which], recv_sem.at[which],
            device_id=to, device_id_type=MESH,
        ).start()

    def each(count, action):
        def turn(index, carry):
            action(index)
            return carry

        lax.fori_loop(0, count, turn, 0, unroll=True)

    def await_bytes(ref, sem):
        pltpu.make_async_copy(ref, ref, sem).wait()

    def arrived(which):
        await_bytes(groups[which], recv_sem.at[which])

    own = [
        pltpu.make_async_copy(ints, ibuf.at[4:28, 0:8], local_sem.at[0]),
        pltpu.make_async_copy(labels, lbuf.at[4:28, 0:8], local_sem.at[1]),
    ]
    for copy in own:
        copy.start()
    barrier = pltpu.get_barrier_semaphore()

    def greet(to):
        pl.semaphore_signal(barrier, inc=1, device_id=to, device_id_type=MESH)

    for dx, dy in MIDDLE:
        greet(device(dx, dy))
    each(31, lambda k: greet(in_column(k)))
    each(15, lambda k: greet(in_plane(k)))
    p2[:, 6:12, :] = jnp.ones((18, 6, BZ), f32)
    x2[:, 6:12, :] = jnp.zeros((18, 6, BZ), f32)
    pl.semaphore_wait(barrier, len(MIDDLE) + 15 + 31)

    for copy in own:
        copy.wait()

    def send_inputs(target, which, pairs, depth, corner_x, corner_y):
        for dx, dy in pairs:
            n, m = (corner_x, corner_y) if dx and dy else (depth, depth)
            sx, tx = {1: (28 - n, 4 - n), -1: (4, 28), 0: (4, 4)}[dx]
            sy, ty = {1: (8 - m, 16 - m), -1: (0, 8), 0: (0, 0)}[dy]
            nx, ny = n if dx else 24, m if dy else 8
            send(
                target.at[sx : sx + nx, sy : sy + ny], target.at[tx : tx + nx, ty : ty + ny],
                which, device(dx, dy),
            )

    aside = [d for d in NEAR if d[0] == 0]
    ahead = [(1, 0), (-1, 0), (1, 1), (1, -1), (-1, 1), (-1, -1)]
    send_inputs(ibuf, 11, ahead, 4, 3, 4)
    send_inputs(lbuf, 12, ahead, 3, 2, 2)
    send_inputs(ibuf, 0, aside, 4, 3, 4)
    send_inputs(lbuf, 1, aside, 3, 2, 2)
    groups[0], groups[1] = ibuf.at[0:12], lbuf.at[0:9]
    groups[11], groups[12] = ibuf.at[0:7], lbuf.at[0:4]
    arrived(0)
    arrived(1)

    def fine_operator(at, count):
        wide = ibuf[pl.ds(at - 1, count + 2)].astype(f32)
        lab = lbuf[pl.ds(at, count)]
        c = wide[1:-1]
        px = weight(wide[1:], wide[:-1])
        gone_x = gx * BX + (at - 5) + place(px.shape, 0)
        px = jnp.where((gone_x == GX * BX - 1) | (gone_x == -1), 0.0, px)
        row = place(c.shape, 1)
        gone_y = gy * BY + jnp.where(row >= 12, row - 16, row)
        py = jnp.where((gone_y == GY * BY - 1) | (gone_y == -1), 0.0, weight(up(c, 1, 1), c))
        my = down(py, 1, 1)
        pz = jnp.where(place(c.shape, 2) == BZ - 1, 0.0, weight(up(c, 1, 2), c))
        mz = down(pz, 1, 2)
        mass = base_mass + jnp.where(lab > 0, seed_gamma, 0.0)
        diagonal, scale = normalise(px[1:], px[:-1], py, my, pz, mz, mass, w0, at, count)
        b0[pl.ds(at, count)] = jnp.where(lab == 1, seed_gamma, 0.0) * scale
        d0[pl.ds(at, count)] = diagonal[:, 0:8] * (1.0 / damping)
        for slot, value in enumerate((px[1:], py, my, pz, mass)):
            fine[slot, pl.ds(at, count)] = value[:, 0:8]

    def level_1(first, last):
        at, end = 4 + 2 * first, 6 + 2 * last
        return coarsen((fine[0, at - 1 : end], *(fine[slot, at:end] for slot in range(1, 5))), 1)

    def packed_1(operator):
        px, py, _, pz, mass = operator
        ybit, zbit = odd(py, 1, 1), odd(py, 1, 2)
        return jnp.where(ybit, jnp.where(zbit, mass, pz), jnp.where(zbit, py, px[1:]))

    def send_1(ref, which, near, whole, corners, ends):
        for dx, dy in MIDDLE:
            if abs(dy) == 2:
                parts = [(*{1: (4, 20), -1: (0, 16)}[dy // 2], 4, corners[2])]
            elif dx and dy and corners[0] == corners[1]:
                parts = [(0, {1: 24, -1: 8}[dy], 8, corners[0])]
            elif dx and dy:
                close, far = {1: ((4, 28), (0, 24)), -1: ((0, 8), (4, 12))}[dy]
                parts = [(*close, 4, corners[0]), (*far, 4, corners[1])]
            else:
                parts = [(0, {0: 0, 1: 24, -1: 8}[dy], 8, near)]
            for sy, ty, ny, n in parts:
                nx = n - ends if dx else whole - 2 * ends
                sx = near + {1: whole - n, -1: ends, 0: ends}[dx]
                tx = {1: near - n, -1: near + whole + ends, 0: near + ends}[dx]
                if nx > 0:
                    send(
                        ref.at[sx : sx + nx, sy : sy + ny], ref.at[tx : tx + nx, ty : ty + ny],
                        which, device(dx, dy),
                    )

    for at in (5, 16):
        fine_operator(at, 11)
    inner = level_1(1, 10)
    p1[7:17, 0:8, :] = packed_1(inner)
    send_1(p1, 2, 6, 12, (5, 3, 1), 1)
    groups[2] = p1.at[0:13]
    sweep(b0, va0, 6, 25, 4, w0, b0, 1, 1)
    arrived(11)
    arrived(12)
    fine_operator(1, 4)
    fine_operator(27, 4)

    lower, upper = level_1(0, 0), level_1(11, 11)
    b1p[3:4, 0:8, :] = packed_1(lower)
    b1p[8:9, 0:8, :] = packed_1(upper)
    op1 = (
        jnp.concatenate([lower[0][0:1], inner[0], upper[0][1:2]], axis=0),
        *(jnp.concatenate(parts, axis=0) for parts in zip(lower[1:], inner[1:], upper[1:])),
    )
    s1[...] = damping / own_diagonal(op1, 2)

    sweep(b0, va0, 2, 5, 4, w0, b0, 1, 1)
    sweep(b0, va0, 26, 29, 4, w0, b0, 1, 1)

    def residual_0(index, carry):
        at = 4 + 6 * index
        here, total = step(va0, at, 6, w0, b0, 1, 1, 8)
        r = pair_x(d0[pl.ds(at, 6)] * (total - here))
        r = pair(pair(r, 1, 1), 1, 2) * s1[pl.ds(3 * index, 3)]
        ybit, zbit = odd(r[0:1], 1, 1), odd(r[0:1], 1, 2)
        b1p[pl.ds(4 + index, 1), 0:8, :] = jnp.where(zbit, jnp.where(ybit, r[2:3], r[1:2]), r[0:1])
        return carry

    lax.fori_loop(0, 4, residual_0, 0, unroll=True)
    send_1(b1p, 3, 3, 6, (3, 3, 2), 0)
    groups[3] = b1p.at[0:10]

    op2 = coarsen(op1, 2)
    px, py, _, pz, mass = op2
    slot = place(py.shape, 2) % 4
    packed = jnp.where(slot == 0, px[1:], jnp.where(slot == 1, py, jnp.where(slot == 2, pz, mass)))
    p2[6:12, 0:2, :] = jnp.where(place(packed.shape, 1) == 0, packed, up(packed, 3, 1))[:, 0:2]

    def send_2(ref, which):
        for dx, dy in MIDDLE:
            n = 6 if dx == 0 else 2 if abs(dy) == 2 else 4
            sx = 12 - n if dx == 1 else 6
            tx = {1: 6 - n, -1: 12, 0: 6}[dx]
            ty = -2 * dy % 16
            send(ref.at[sx : sx + n, 0:2], ref.at[tx : tx + n, ty : ty + 2], which, device(dx, dy))
        groups[which] = ref.at[0:7]

    send_2(p2, 4)

    op3 = coarsen(op2, 4)
    s3 = damping / own_diagonal(op3, 8)
    px, py, _, pz, mass = op3
    for index, value in enumerate((px[1:], py, pz, mass)):
        o3[3 * index : 3 * index + 3] = value

    def gather_plane(source, target, which):
        seat = core * 8 + chip_y
        target[:, pl.ds(seat, 1), :] = source[:, 0:1, :]
        each(15, lambda k: send(source.at[:, 0:1], target.at[:, pl.ds(seat, 1)], which, in_plane(k)))
        groups[which] = target.at[:, 0:15]

    def merge(source, target, kinds):
        rows = source[...]
        rows = jnp.where(place(rows.shape, 2) % 8 == place(rows.shape, 1) % 8, rows, 0.0)
        rows = rows.reshape(3 * kinds * 2, 8, BZ)
        for distance in (1, 2, 4):
            rows = rows + up(rows, distance, 1)
        target[...] = rows.reshape(kinds, 3, 2, 8, BZ)

    def gather_column(source, target, which, kinds):
        piece = source.at[kinds, :, :, 0:1]
        seat = target.at[kinds, half, :, pl.ds(gy % 4 // 2 * 2, 2), pl.ds(gy // 4, 1)]
        pltpu.make_async_copy(piece, seat, recv_sem.at[which]).start()
        each(31, lambda k: send(piece, seat, which, in_column(k)))

    gather_plane(o3, g1o, 6)

    arrived(2)

    def weights_1(at, count):
        packed = p1[at - 1 : at + count]
        even_z, odd_z = low(packed, 1, 2), high(packed[1:], 1, 2)
        px, pz = low(even_z, 1, 1), high(even_z[1:], 1, 1)
        py, mass = low(odd_z, 1, 1), high(odd_z, 1, 1)
        diagonal, _ = normalise(px[1:], px[:-1], py, down(py, 2, 1), pz, down(pz, 2, 2), mass, w1, at, count)
        d1[at : at + count] = diagonal * (1.0 / damping)

    for at, count in ((1, 4), (8, 3), (11, 3), (14, 3), (20, 3)):
        weights_1(at, count)
    arrived(3)
    for plane, end in ((5, 2), (6, 3), (17, 8), (18, 9)):
        p1[plane] = b1p[end]
    for at in (5, 17):
        weights_1(at, 3)
    for index, plane in enumerate((0, 1, 4, 5, 6, 7, 10, 11)):
        packed = b1p[plane : plane + 1]
        odd_z = high(packed, 1, 2)
        b1[3 * index : 3 * index + 1] = low(packed, 1, 2)
        b1[3 * index + 1 : 3 * index + 2] = low(odd_z, 1, 1)
        b1[3 * index + 2 : 3 * index + 3] = high(odd_z, 1, 1)
    sweep(b1, va1, 1, 22, 2, w1, b1, 2, 2)

    def residual_1(index, carry):
        at = 2 + 4 * index
        here, total = step(va1, at, 4, w1, b1, 2, 2)
        r = pair_x(d1[pl.ds(at, 4)] * (total - here))
        r = pair(pair(r, 2, 1), 2, 2)
        mine, after, before = r[:, 0:8], r[:, 8:16], r[:, 24:32]
        row = place(mine.shape, 1)
        first = jnp.where(row < 2, jnp.where(row == 0, mine, up(mine, 3, 1)), jnp.where(row == 2, down(after, 2, 1), up(after, 1, 1)))
        last = jnp.where(row == 7, down(before, 3, 1), up(before, 2, 1))
        to = pl.ds(4 + 2 * index, 2)
        b2[to, 0:8, :] = first
        b2[to, 8:16, :] = last
        return carry

    lax.fori_loop(0, 5, residual_1, 0, unroll=True)

    arrived(4)

    def weights_2(index, carry):
        at = 1 + 4 * index
        packed = p2[pl.ds(at - 1, 5)]
        even_z, odd_z = low(packed, 1, 2), high(packed[1:], 1, 2)
        px, pz = low(even_z, 2, 2), high(even_z[1:], 2, 2)
        py, mass = low(odd_z, 2, 2), high(odd_z, 2, 2)
        diagonal, scale = normalise(px[1:], px[:-1], py, down(py, 1, 1), pz, down(pz, 4, 2), mass, w2, at, 4)
        d2[pl.ds(at, 4)] = diagonal * (1.0 / damping)
        s2[pl.ds(at, 4)] = scale
        return carry

    lax.fori_loop(0, 4, weights_2, 0, unroll=True)
    b2[4:14] = b2[4:14] * s2[4:14]

    sweep(b2, va2, 5, 12, 4, w2, b2, 1, 4)
    here, total = step(va2, 6, 6, w2, b2, 1, 4, 8)
    r = pair_x(d2[6:12, 0:8, :] * (total - here))
    r = pair(pair(r, 1, 1), 4, 2)
    o4[...] = r * s3
    gather_plane(o4, g1, 8)

    arrived(6)
    merge(g1o, qo, 4)
    half_kinds = pl.ds(2 * core, 2)
    gather_column(qo, g2o, 7, half_kinds)
    groups[7] = g2o.at[0:2]
    zbit = odd(here[:, 0:2], 1, 2)
    x2[6:12, 0:2, :] = jnp.where(zbit, b2[6:12, 0:2, :], here[:, 0:2])
    send_2(x2, 5)

    arrived(8)
    merge(g1, q, 1)
    gather_column(q, g2, 9, pl.ds(0, 1))
    groups[9] = g2

    arrived(7)
    send(g2o.at[half_kinds], g2o.at[half_kinds], 10, (gx, gy + 1 - 2 * core))
    groups[10] = g2o.at[0:2]
    arrived(5)
    b2[...] = high(x2[...], 1, 2)
    va2[...] = low(x2[...], 1, 2)

    whole = (3, 4, 2, 8, BZ)

    def lanes(v, shift):
        return pltpu.roll(v.reshape(-1, 8, BZ), shift, 2).reshape(v.shape)

    def rows(v, shift):
        return pltpu.roll(v.reshape(-1, 8, BZ), shift, 1).reshape(v.shape)

    def spread(v):
        second = odd(v[0], 8, 3)
        return jnp.stack(
            [jnp.where(second, lanes(v[1], 8), v[0]), jnp.where(second, v[1], lanes(v[0], BZ - 8))],
            axis=2,
        )

    def around(v):
        return (
            jnp.concatenate([v[1:], lanes(v[:1], BZ - 1)], axis=0),
            jnp.concatenate([lanes(v[2:], 1), v[:2]], axis=0),
            jnp.concatenate([v[:, 1:], rows(v[:, :1], 7)], axis=1),
            jnp.concatenate([rows(v[:, 3:], 1), v[:, :3]], axis=1),
            jnp.concatenate([v[:, :, 1:], lanes(v[:, :, :1], BZ - 16)], axis=2),
            jnp.concatenate([lanes(v[:, :, 1:], 16), v[:, :, :1]], axis=2),
        )

    arrived(10)
    px, py, pz, mass = [spread(g2o[k]) for k in range(4)]
    mx, my, mz = around(px)[1], around(py)[3], around(pz)[5]
    scale = damping / (mass + px + mx + py + my + pz + mz)
    for index, value in enumerate((px, mx, py, my, pz, mz)):
        w3[index] = value * scale
    arrived(9)
    b3[...] = spread(g2[0])

    def solve(index, v):
        total = (1.0 - damping) * v + b3[...]
        for k, n in enumerate(around(v)):
            total = total + w3[k] * n
        return total

    solved[...] = lax.fori_loop(1, COARSE_ITERS, solve, b3[...], unroll=True)

    row = (place((16, BZ), 0) // 2 + 2) % 8
    slot = place((16, BZ), 1) % 16
    for j in range(-2, 5):
        at = (3 * gx + j + 48) % 48
        tiles = []
        for z_low in range(2):
            tile = jnp.zeros((16, BZ), f32)
            for k in range(-2, 3):
                y = (gy + k + GY) % GY
                line = solved[pl.ds(at % 3, 1), pl.ds(y % 4, 1), z_low, pl.ds(y // 4, 1), :]
                tile = jnp.where(row == k + 2, line.reshape(1, BZ), tile)
            tiles.append(pair(jnp.where(slot == at // 3, tile, 0.0), 8, 1))
        tile = jnp.where(slot >= 8, tiles[1], tiles[0])
        tile = pair(pair(pair(tile, 1, 1), 2, 1), 4, 1)
        va2[6 + 2 * j : 8 + 2 * j] = va2[6 + 2 * j : 8 + 2 * j] + tile[None]
    sweep(va2, vb2, 3, 14, 4, w2, b2, 1, 4)
    sweep(vb2, va2, 4, 13, 5, w2, b2, 1, 4)

    second = place((1, 8, BZ), 1) >= 4

    def correct_1(index, carry):
        for rows, first in ((0, 0), (8, 2), (24, 14)):
            a = va2[pl.ds(4 + index, 1), first : first + 1, :]
            b = va2[pl.ds(4 + index, 1), first + 1 : first + 2, :]
            at = pl.ds(2 + 2 * index, 2)
            va1[at, rows : rows + 8, :] = va1[at, rows : rows + 8, :] + jnp.where(second, b, a)
        return carry

    lax.fori_loop(0, 10, correct_1, 0, unroll=True)
    sweep(va1, vb1, 4, 19, 2, w1, b1, 2, 2)
    sweep(vb1, va1, 5, 18, 2, w1, b1, 2, 2)

    def correct_0(index, carry):
        at = pl.ds(2 + 2 * index, 2)
        coarse = va1[pl.ds(5 + index, 1)]
        va0[at, 0:8, :] = va0[at, 0:8, :] + coarse[:, 0:8]
        va0[at, 8:16, :] = va0[at, 8:16, :] + jnp.where(second, coarse[:, 24:32], coarse[:, 8:16])
        return carry

    lax.fori_loop(0, 14, correct_0, 0, unroll=True)
    sweep(va0, vb0, 2, 29, 4, w0, b0, 1, 1)

    for at in (0, 8, 16):
        _, total = step(vb0, 4 + at, 8, w0, b0, 1, 1, 8)
        out[at : at + 8] = total

    for which in (0, 1, 2, 3, 4, 5, 6, 8, 10, 11, 12):
        await_bytes(groups[which], send_sem.at[which])
    await_bytes(p1.at[0:12, 0:31], send_sem.at[7])
    await_bytes(p1.at[0:6, 0:31], send_sem.at[9])


def shards(intensities, labels):
    def vmem(*shape, dtype=f32):
        return pltpu.VMEM(shape, dtype)

    zero, one, two = (32, 16, BZ), (24, 32, BZ), (18, 16, BZ)
    return pl.pallas_call(
        kernel,
        out_shape=jax.ShapeDtypeStruct((BX, BY, BZ), f32),
        in_specs=[pl.BlockSpec(memory_space=pltpu.HBM)] * 2,
        out_specs=pl.BlockSpec(memory_space=pltpu.VMEM),
        scratch_shapes=[
            vmem(*zero, dtype=jnp.int32), vmem(*zero, dtype=jnp.int32),
            [vmem(*zero)] * 6, vmem(*zero), vmem(32, 8, BZ), vmem(5, 32, 8, BZ),
            vmem(*zero), vmem(*zero),
            vmem(*one), vmem(12, 32, BZ), vmem(*one), [vmem(*one)] * 6, vmem(*one), vmem(12, 8, BZ),
            vmem(*one), vmem(*one),
            vmem(*two), vmem(*two), vmem(*two), [vmem(*two)] * 6, vmem(*two), vmem(*two),
            vmem(*two), vmem(*two),
            vmem(12, 8, BZ), vmem(12, 16, BZ), vmem(4, 3, 2, 8, BZ), vmem(4, 2, 3, 4, 8, BZ),
            vmem(3, 8, BZ), vmem(3, 16, BZ), vmem(1, 3, 2, 8, BZ), vmem(1, 2, 3, 4, 8, BZ),
            vmem(6, 3, 4, 2, 8, BZ), vmem(3, 4, 2, 8, BZ), vmem(3, 4, 2, 8, BZ),
            pltpu.SemaphoreType.DMA((2,)),
            pltpu.SemaphoreType.DMA((13,)),
            pltpu.SemaphoreType.DMA((13,)),
        ],
        compiler_params=pltpu.CompilerParams(
            collective_id=0, has_side_effects=True, vmem_limit_bytes=55125 * 1024
        ),
        name="v_cycle",
    )(intensities, labels)


def solution(mesh):
    return jax.shard_map(
        shards,
        mesh=mesh,
        in_specs=(P("gx", "gy", None), P("gx", "gy", None)),
        out_specs=P("gx", "gy", None),
        check_vma=False,
    )
```

```python
import jax
import jax.numpy as jnp
from jax import lax
from jax.experimental import pallas as pl
from jax.experimental.pallas import tpu as pltpu
from jax.sharding import PartitionSpec as P

COARSE_ITERS = 30

edge_beta = 3.0
seed_gamma = 4.0
base_mass = 0.1
damping = 0.7

MESH = pl.DeviceIdType.MESH
f32 = jnp.float32

BX, BY, BZ = 24, 8, 128
GX, GY = 16, 32

NEAR = [(dx, dy) for dx in (-1, 0, 1) for dy in (-1, 0, 1) if (dx, dy) != (0, 0)]
MIDDLE = [(dx, dy) for dx in (-1, 1, 0) for dy in (0, -1, 1, -2, 2) if (dx, dy) != (0, 0)]


def place(shape, axis):
    return lax.broadcasted_iota(jnp.int32, shape, axis)


def up(array, distance, axis):
    return pltpu.roll(array, array.shape[axis] - distance, axis)


def down(array, distance, axis):
    return pltpu.roll(array, distance, axis)


def odd(array, distance, axis):
    return (place(array.shape, axis) // distance) % 2 == 1


def high(array, distance, axis):
    return jnp.where(odd(array, distance, axis), array, up(array, distance, axis))


def low(array, distance, axis):
    return jnp.where(odd(array, distance, axis), down(array, distance, axis), array)


def pair(array, distance, axis):
    return array + jnp.where(
        odd(array, distance, axis), down(array, distance, axis), up(array, distance, axis)
    )


def halves(array):
    split = array.reshape((array.shape[0] // 2, 2) + array.shape[1:])
    return split[:, 0], split[:, 1]


def pair_x(array):
    first, second = halves(array)
    return first + second


def coarsen(operator, distance):
    px, py, my, pz, mass = operator
    next_px = jnp.concatenate([px[0:1], halves(px[1:])[1]], axis=0)
    next_px = pair(pair(next_px, distance, 1), distance, 2)
    next_py = high(pair(pair_x(py), distance, 2), distance, 1)
    next_my = low(pair(pair_x(my), distance, 2), distance, 1)
    next_pz = high(pair(pair_x(pz), distance, 1), distance, 2)
    next_mass = pair(pair(pair_x(mass), distance, 1), distance, 2)
    return next_px, next_py, next_my, next_pz, next_mass


def own_diagonal(operator, distance):
    px, py, my, pz, mass = operator
    return mass + px[1:] + px[:-1] + py + my + pz + down(pz, distance, 2)


def weight(upper, lower):
    gap = upper - lower
    return jnp.exp(gap * gap * (-edge_beta / (255.0 * 255.0)))


def step(source, first, count, weights, rhs, dist_y, dist_z, rows=None):
    v = source[pl.ds(first - 1, count + 2)]
    c = v[1:-1]
    near = [v[2:], v[:-2], up(c, dist_y, 1), down(c, dist_y, 1), up(c, dist_z, 2), down(c, dist_z, 2)]
    rows = c.shape[1] if rows is None else rows
    here = c[:, :rows]
    total = (1.0 - damping) * here + rhs[pl.ds(first, count), 0:rows, :]
    for w, n in zip(weights, near):
        total = total + w[pl.ds(first, count), 0:rows, :] * n[:, :rows]
    return here, total


def sweep(source, target, first, last, count, weights, rhs, dist_y, dist_z):
    def turn(index, carry):
        at = first + index * count
        _, total = step(source, at, count, weights, rhs, dist_y, dist_z)
        target[pl.ds(at, count)] = total
        return carry

    lax.fori_loop(0, (last + 1 - first) // count, turn, 0, unroll=True)


def normalise(px, px_before, py, my, pz, mz, mass, stores, at, count):
    diagonal = mass + px + px_before + py + my + pz + mz
    scale = damping / diagonal
    for store, value in zip(stores, (px, px_before, py, my, pz, mz)):
        store[pl.ds(at, count)] = value * scale
    return diagonal, scale


def kernel(
    ints, labels, out,
    ibuf, lbuf, w0, b0, d0, fine, va0, vb0,
    p1, b1p, b1, w1, d1, s1, va1, vb1,
    p2, x2, b2, w2, d2, s2, va2, vb2,
    o3, g1o, qo, g2o, o4, g1, q, g2, w3, b3, solved,
    local_sem, send_sem, recv_sem,
):
    gx, gy = lax.axis_index("gx"), lax.axis_index("gy")
    half, chip_y = gx // 8, gx % 8
    chip_z, chip_x, core = half * 4 + gy // 8, gy % 8 // 2, gy % 2
    groups = {}

    def device(dx, dy):
        return (lax.rem(gx + dx + GX, GX), lax.rem(gy + dy + GY, GY))

    def offset(k, size):
        return (size // 2 + (k + 1) // 2 * (1 - 2 * (k % 2))) % size

    def in_plane(k):
        return (half * 8 + (chip_y + offset(k // 2, 8)) % 8, gy - core + (core + k + 1) % 2)

    def in_column(k):
        z = (chip_z + offset(k // 4, 8)) % 8
        x = (chip_x + offset(k % 4, 4)) % 4
        return (z // 4 * 8 + chip_y, z % 4 * 8 + x * 2 + core)

    def send(source, target, which, to):
        pltpu.make_async_remote_copy(
            source, target, send_sem.at[which], recv_sem.at[which],
            device_id=to, device_id_type=MESH,
        ).start()

    def each(count, action):
        def turn(index, carry):
            action(index)
            return carry

        lax.fori_loop(0, count, turn, 0, unroll=True)

    def await_bytes(ref, sem):
        pltpu.make_async_copy(ref, ref, sem).wait()

    def arrived(which):
        await_bytes(groups[which], recv_sem.at[which])

    own = [
        pltpu.make_async_copy(ints, ibuf.at[4:28, 0:8], local_sem.at[0]),
        pltpu.make_async_copy(labels, lbuf.at[4:28, 0:8], local_sem.at[1]),
    ]
    for copy in own:
        copy.start()
    barrier = pltpu.get_barrier_semaphore()

    def greet(to):
        pl.semaphore_signal(barrier, inc=1, device_id=to, device_id_type=MESH)

    for dx, dy in MIDDLE:
        greet(device(dx, dy))
    each(31, lambda k: greet(in_column(k)))
    each(15, lambda k: greet(in_plane(k)))
    p2[:, 6:12, :] = jnp.ones((18, 6, BZ), f32)
    x2[:, 6:12, :] = jnp.zeros((18, 6, BZ), f32)
    pl.semaphore_wait(barrier, len(MIDDLE) + 15 + 31)

    for copy in own:
        copy.wait()

    def send_inputs(target, which, pairs, depth, corner_x, corner_y):
        for dx, dy in pairs:
            n, m = (corner_x, corner_y) if dx and dy else (depth, depth)
            sx, tx = {1: (28 - n, 4 - n), -1: (4, 28), 0: (4, 4)}[dx]
            sy, ty = {1: (8 - m, 16 - m), -1: (0, 8), 0: (0, 0)}[dy]
            nx, ny = n if dx else 24, m if dy else 8
            send(
                target.at[sx : sx + nx, sy : sy + ny], target.at[tx : tx + nx, ty : ty + ny],
                which, device(dx, dy),
            )

    aside = [d for d in NEAR if d[0] == 0]
    ahead = [(1, 0), (-1, 0), (1, 1), (1, -1), (-1, 1), (-1, -1)]
    send_inputs(ibuf, 11, ahead, 4, 3, 4)
    send_inputs(lbuf, 12, ahead, 3, 2, 2)
    send_inputs(ibuf, 0, aside, 4, 3, 4)
    send_inputs(lbuf, 1, aside, 3, 2, 2)
    groups[0], groups[1] = ibuf.at[0:12], lbuf.at[0:9]
    groups[11], groups[12] = ibuf.at[0:7], lbuf.at[0:4]
    arrived(0)
    arrived(1)

    def fine_operator(at, count):
        wide = ibuf[pl.ds(at - 1, count + 2)].astype(f32)
        lab = lbuf[pl.ds(at, count)]
        c = wide[1:-1]
        px = weight(wide[1:], wide[:-1])
        gone_x = gx * BX + (at - 5) + place(px.shape, 0)
        px = jnp.where((gone_x == GX * BX - 1) | (gone_x == -1), 0.0, px)
        row = place(c.shape, 1)
        gone_y = gy * BY + jnp.where(row >= 12, row - 16, row)
        py = jnp.where((gone_y == GY * BY - 1) | (gone_y == -1), 0.0, weight(up(c, 1, 1), c))
        my = down(py, 1, 1)
        pz = jnp.where(place(c.shape, 2) == BZ - 1, 0.0, weight(up(c, 1, 2), c))
        mz = down(pz, 1, 2)
        mass = base_mass + jnp.where(lab > 0, seed_gamma, 0.0)
        diagonal, scale = normalise(px[1:], px[:-1], py, my, pz, mz, mass, w0, at, count)
        b0[pl.ds(at, count)] = jnp.where(lab == 1, seed_gamma, 0.0) * scale
        d0[pl.ds(at, count)] = diagonal[:, 0:8] * (1.0 / damping)
        for slot, value in enumerate((px[1:], py, my, pz, mass)):
            fine[slot, pl.ds(at, count)] = value[:, 0:8]

    def level_1(first, last):
        at, end = 4 + 2 * first, 6 + 2 * last
        return coarsen((fine[0, at - 1 : end], *(fine[slot, at:end] for slot in range(1, 5))), 1)

    def packed_1(operator):
        px, py, _, pz, mass = operator
        ybit, zbit = odd(py, 1, 1), odd(py, 1, 2)
        return jnp.where(ybit, jnp.where(zbit, mass, pz), jnp.where(zbit, py, px[1:]))

    def send_1(ref, which, near, whole, corners, ends):
        for dx, dy in MIDDLE:
            if abs(dy) == 2:
                parts = [(*{1: (4, 20), -1: (0, 16)}[dy // 2], 4, corners[2])]
            elif dx and dy and corners[0] == corners[1]:
                parts = [(0, {1: 24, -1: 8}[dy], 8, corners[0])]
            elif dx and dy:
                close, far = {1: ((4, 28), (0, 24)), -1: ((0, 8), (4, 12))}[dy]
                parts = [(*close, 4, corners[0]), (*far, 4, corners[1])]
            else:
                parts = [(0, {0: 0, 1: 24, -1: 8}[dy], 8, near)]
            for sy, ty, ny, n in parts:
                nx = n - ends if dx else whole - 2 * ends
                sx = near + {1: whole - n, -1: ends, 0: ends}[dx]
                tx = {1: near - n, -1: near + whole + ends, 0: near + ends}[dx]
                if nx > 0:
                    send(
                        ref.at[sx : sx + nx, sy : sy + ny], ref.at[tx : tx + nx, ty : ty + ny],
                        which, device(dx, dy),
                    )

    for at in (5, 16):
        fine_operator(at, 11)
    inner = level_1(1, 10)
    p1[7:17, 0:8, :] = packed_1(inner)
    send_1(p1, 2, 6, 12, (5, 3, 1), 1)
    groups[2] = p1.at[0:13]
    sweep(b0, va0, 6, 25, 4, w0, b0, 1, 1)
    arrived(11)
    arrived(12)
    fine_operator(1, 4)
    fine_operator(27, 4)

    lower, upper = level_1(0, 0), level_1(11, 11)
    b1p[3:4, 0:8, :] = packed_1(lower)
    b1p[8:9, 0:8, :] = packed_1(upper)
    op1 = (
        jnp.concatenate([lower[0][0:1], inner[0], upper[0][1:2]], axis=0),
        *(jnp.concatenate(parts, axis=0) for parts in zip(lower[1:], inner[1:], upper[1:])),
    )
    s1[...] = damping / own_diagonal(op1, 2)

    sweep(b0, va0, 2, 5, 4, w0, b0, 1, 1)
    sweep(b0, va0, 26, 29, 4, w0, b0, 1, 1)

    def residual_0(index, carry):
        at = 4 + 6 * index
        here, total = step(va0, at, 6, w0, b0, 1, 1, 8)
        r = pair_x(d0[pl.ds(at, 6)] * (total - here))
        r = pair(pair(r, 1, 1), 1, 2) * s1[pl.ds(3 * index, 3)]
        ybit, zbit = odd(r[0:1], 1, 1), odd(r[0:1], 1, 2)
        b1p[pl.ds(4 + index, 1), 0:8, :] = jnp.where(zbit, jnp.where(ybit, r[2:3], r[1:2]), r[0:1])
        return carry

    lax.fori_loop(0, 4, residual_0, 0, unroll=True)
    send_1(b1p, 3, 3, 6, (3, 3, 2), 0)
    groups[3] = b1p.at[0:10]

    op2 = coarsen(op1, 2)
    px, py, _, pz, mass = op2
    slot = place(py.shape, 2) % 4
    packed = jnp.where(slot == 0, px[1:], jnp.where(slot == 1, py, jnp.where(slot == 2, pz, mass)))
    p2[6:12, 0:2, :] = jnp.where(place(packed.shape, 1) == 0, packed, up(packed, 3, 1))[:, 0:2]

    def send_2(ref, which):
        for dx, dy in MIDDLE:
            n = 6 if dx == 0 else 2 if abs(dy) == 2 else 4
            sx = 12 - n if dx == 1 else 6
            tx = {1: 6 - n, -1: 12, 0: 6}[dx]
            ty = -2 * dy % 16
            send(ref.at[sx : sx + n, 0:2], ref.at[tx : tx + n, ty : ty + 2], which, device(dx, dy))
        groups[which] = ref.at[0:7]

    op3 = coarsen(op2, 4)
    s3 = damping / own_diagonal(op3, 8)
    px, py, _, pz, mass = op3
    for index, value in enumerate((px[1:], py, pz, mass)):
        o3[3 * index : 3 * index + 3] = value

    def gather_plane(source, target, which):
        seat = core * 8 + chip_y
        target[:, pl.ds(seat, 1), :] = source[:, 0:1, :]
        each(15, lambda k: send(source.at[:, 0:1], target.at[:, pl.ds(seat, 1)], which, in_plane(k)))
        groups[which] = target.at[:, 0:15]

    def merge(source, target, kinds):
        rows = source[...]
        rows = jnp.where(place(rows.shape, 2) % 8 == place(rows.shape, 1) % 8, rows, 0.0)
        rows = rows.reshape(3 * kinds * 2, 8, BZ)
        for distance in (1, 2, 4):
            rows = rows + up(rows, distance, 1)
        target[...] = rows.reshape(kinds, 3, 2, 8, BZ)

    def gather_column(source, target, which, kinds):
        piece = source.at[kinds, :, :, 0:1]
        seat = target.at[kinds, half, :, pl.ds(gy % 4 // 2 * 2, 2), pl.ds(gy // 4, 1)]
        pltpu.make_async_copy(piece, seat, recv_sem.at[which]).start()
        each(31, lambda k: send(piece, seat, which, in_column(k)))

    gather_plane(o3, g1o, 6)
    send_2(p2, 4)

    arrived(2)

    def weights_1(at, count):
        packed = p1[at - 1 : at + count]
        even_z, odd_z = low(packed, 1, 2), high(packed[1:], 1, 2)
        px, pz = low(even_z, 1, 1), high(even_z[1:], 1, 1)
        py, mass = low(odd_z, 1, 1), high(odd_z, 1, 1)
        diagonal, _ = normalise(px[1:], px[:-1], py, down(py, 2, 1), pz, down(pz, 2, 2), mass, w1, at, count)
        d1[at : at + count] = diagonal * (1.0 / damping)

    for at, count in ((1, 4), (8, 3), (11, 3), (14, 3), (20, 3)):
        weights_1(at, count)
    arrived(6)
    merge(g1o, qo, 4)
    half_kinds = pl.ds(2 * core, 2)
    gather_column(qo, g2o, 7, half_kinds)
    groups[7] = g2o.at[0:2]
    arrived(3)
    for plane, end in ((5, 2), (6, 3), (17, 8), (18, 9)):
        p1[plane] = b1p[end]
    for at in (5, 17):
        weights_1(at, 3)
    for index, plane in enumerate((0, 1, 4, 5, 6, 7, 10, 11)):
        packed = b1p[plane : plane + 1]
        odd_z = high(packed, 1, 2)
        b1[3 * index : 3 * index + 1] = low(packed, 1, 2)
        b1[3 * index + 1 : 3 * index + 2] = low(odd_z, 1, 1)
        b1[3 * index + 2 : 3 * index + 3] = high(odd_z, 1, 1)
    sweep(b1, va1, 1, 22, 2, w1, b1, 2, 2)

    def residual_1(index, carry):
        at = 2 + 4 * index
        here, total = step(va1, at, 4, w1, b1, 2, 2)
        r = pair_x(d1[pl.ds(at, 4)] * (total - here))
        r = pair(pair(r, 2, 1), 2, 2)
        mine, after, before = r[:, 0:8], r[:, 8:16], r[:, 24:32]
        row = place(mine.shape, 1)
        first = jnp.where(row < 2, jnp.where(row == 0, mine, up(mine, 3, 1)), jnp.where(row == 2, down(after, 2, 1), up(after, 1, 1)))
        last = jnp.where(row == 7, down(before, 3, 1), up(before, 2, 1))
        to = pl.ds(4 + 2 * index, 2)
        b2[to, 0:8, :] = first
        b2[to, 8:16, :] = last
        return carry

    lax.fori_loop(0, 5, residual_1, 0, unroll=True)

    arrived(4)

    def weights_2(index, carry):
        at = 1 + 4 * index
        packed = p2[pl.ds(at - 1, 5)]
        even_z, odd_z = low(packed, 1, 2), high(packed[1:], 1, 2)
        px, pz = low(even_z, 2, 2), high(even_z[1:], 2, 2)
        py, mass = low(odd_z, 2, 2), high(odd_z, 2, 2)
        diagonal, scale = normalise(px[1:], px[:-1], py, down(py, 1, 1), pz, down(pz, 4, 2), mass, w2, at, 4)
        d2[pl.ds(at, 4)] = diagonal * (1.0 / damping)
        s2[pl.ds(at, 4)] = scale
        return carry

    lax.fori_loop(0, 4, weights_2, 0, unroll=True)
    b2[4:14] = b2[4:14] * s2[4:14]

    sweep(b2, va2, 5, 12, 4, w2, b2, 1, 4)
    here, total = step(va2, 6, 6, w2, b2, 1, 4, 8)
    r = pair_x(d2[6:12, 0:8, :] * (total - here))
    r = pair(pair(r, 1, 1), 4, 2)
    o4[...] = r * s3
    gather_plane(o4, g1, 8)

    zbit = odd(here[:, 0:2], 1, 2)
    x2[6:12, 0:2, :] = jnp.where(zbit, b2[6:12, 0:2, :], here[:, 0:2])
    send_2(x2, 5)

    arrived(8)
    merge(g1, q, 1)
    gather_column(q, g2, 9, pl.ds(0, 1))
    groups[9] = g2

    arrived(7)
    send(g2o.at[half_kinds], g2o.at[half_kinds], 10, (gx, gy + 1 - 2 * core))
    groups[10] = g2o.at[0:2]
    arrived(5)
    b2[...] = high(x2[...], 1, 2)
    va2[...] = low(x2[...], 1, 2)

    whole = (3, 4, 2, 8, BZ)

    def lanes(v, shift):
        return pltpu.roll(v.reshape(-1, 8, BZ), shift, 2).reshape(v.shape)

    def rows(v, shift):
        return pltpu.roll(v.reshape(-1, 8, BZ), shift, 1).reshape(v.shape)

    def spread(v):
        second = odd(v[0], 8, 3)
        return jnp.stack(
            [jnp.where(second, lanes(v[1], 8), v[0]), jnp.where(second, v[1], lanes(v[0], BZ - 8))],
            axis=2,
        )

    def around(v):
        return (
            jnp.concatenate([v[1:], lanes(v[:1], BZ - 1)], axis=0),
            jnp.concatenate([lanes(v[2:], 1), v[:2]], axis=0),
            jnp.concatenate([v[:, 1:], rows(v[:, :1], 7)], axis=1),
            jnp.concatenate([rows(v[:, 3:], 1), v[:, :3]], axis=1),
            jnp.concatenate([v[:, :, 1:], lanes(v[:, :, :1], BZ - 16)], axis=2),
            jnp.concatenate([lanes(v[:, :, 1:], 16), v[:, :, :1]], axis=2),
        )

    arrived(10)
    px, py, pz, mass = [spread(g2o[k]) for k in range(4)]
    mx, my, mz = around(px)[1], around(py)[3], around(pz)[5]
    scale = damping / (mass + px + mx + py + my + pz + mz)
    for index, value in enumerate((px, mx, py, my, pz, mz)):
        w3[index] = value * scale
    arrived(9)
    b3[...] = spread(g2[0])

    def solve(index, v):
        total = (1.0 - damping) * v + b3[...]
        for k, n in enumerate(around(v)):
            total = total + w3[k] * n
        return total

    solved[...] = lax.fori_loop(1, COARSE_ITERS, solve, b3[...], unroll=True)

    row = (place((16, BZ), 0) // 2 + 2) % 8
    slot = place((16, BZ), 1) % 16
    for j in range(-2, 5):
        at = (3 * gx + j + 48) % 48
        tiles = []
        for z_low in range(2):
            tile = jnp.zeros((16, BZ), f32)
            for k in range(-2, 3):
                y = (gy + k + GY) % GY
                line = solved[pl.ds(at % 3, 1), pl.ds(y % 4, 1), z_low, pl.ds(y // 4, 1), :]
                tile = jnp.where(row == k + 2, line.reshape(1, BZ), tile)
            tiles.append(pair(jnp.where(slot == at // 3, tile, 0.0), 8, 1))
        tile = jnp.where(slot >= 8, tiles[1], tiles[0])
        tile = pair(pair(pair(tile, 1, 1), 2, 1), 4, 1)
        va2[6 + 2 * j : 8 + 2 * j] = va2[6 + 2 * j : 8 + 2 * j] + tile[None]
    sweep(va2, vb2, 3, 14, 4, w2, b2, 1, 4)
    sweep(vb2, va2, 4, 13, 5, w2, b2, 1, 4)

    second = place((1, 8, BZ), 1) >= 4

    def correct_1(index, carry):
        for rows, first in ((0, 0), (8, 2), (24, 14)):
            a = va2[pl.ds(4 + index, 1), first : first + 1, :]
            b = va2[pl.ds(4 + index, 1), first + 1 : first + 2, :]
            at = pl.ds(2 + 2 * index, 2)
            va1[at, rows : rows + 8, :] = va1[at, rows : rows + 8, :] + jnp.where(second, b, a)
        return carry

    lax.fori_loop(0, 10, correct_1, 0, unroll=True)
    sweep(va1, vb1, 4, 19, 2, w1, b1, 2, 2)
    sweep(vb1, va1, 5, 18, 2, w1, b1, 2, 2)

    def correct_0(index, carry):
        at = pl.ds(2 + 2 * index, 2)
        coarse = va1[pl.ds(5 + index, 1)]
        va0[at, 0:8, :] = va0[at, 0:8, :] + coarse[:, 0:8]
        va0[at, 8:16, :] = va0[at, 8:16, :] + jnp.where(second, coarse[:, 24:32], coarse[:, 8:16])
        return carry

    lax.fori_loop(0, 14, correct_0, 0, unroll=True)
    sweep(va0, vb0, 2, 29, 4, w0, b0, 1, 1)

    for at in (0, 8, 16):
        _, total = step(vb0, 4 + at, 8, w0, b0, 1, 1, 8)
        out[at : at + 8] = total

    for which in (0, 1, 2, 3, 4, 5, 6, 8, 10, 11, 12):
        await_bytes(groups[which], send_sem.at[which])
    await_bytes(p1.at[0:12, 0:31], send_sem.at[7])
    await_bytes(p1.at[0:6, 0:31], send_sem.at[9])


def shards(intensities, labels):
    def vmem(*shape, dtype=f32):
        return pltpu.VMEM(shape, dtype)

    zero, one, two = (32, 16, BZ), (24, 32, BZ), (18, 16, BZ)
    return pl.pallas_call(
        kernel,
        out_shape=jax.ShapeDtypeStruct((BX, BY, BZ), f32),
        in_specs=[pl.BlockSpec(memory_space=pltpu.HBM)] * 2,
        out_specs=pl.BlockSpec(memory_space=pltpu.VMEM),
        scratch_shapes=[
            vmem(*zero, dtype=jnp.int32), vmem(*zero, dtype=jnp.int32),
            [vmem(*zero)] * 6, vmem(*zero), vmem(32, 8, BZ), vmem(5, 32, 8, BZ),
            vmem(*zero), vmem(*zero),
            vmem(*one), vmem(12, 32, BZ), vmem(*one), [vmem(*one)] * 6, vmem(*one), vmem(12, 8, BZ),
            vmem(*one), vmem(*one),
            vmem(*two), vmem(*two), vmem(*two), [vmem(*two)] * 6, vmem(*two), vmem(*two),
            vmem(*two), vmem(*two),
            vmem(12, 8, BZ), vmem(12, 16, BZ), vmem(4, 3, 2, 8, BZ), vmem(4, 2, 3, 4, 8, BZ),
            vmem(3, 8, BZ), vmem(3, 16, BZ), vmem(1, 3, 2, 8, BZ), vmem(1, 2, 3, 4, 8, BZ),
            vmem(6, 3, 4, 2, 8, BZ), vmem(3, 4, 2, 8, BZ), vmem(3, 4, 2, 8, BZ),
            pltpu.SemaphoreType.DMA((2,)),
            pltpu.SemaphoreType.DMA((13,)),
            pltpu.SemaphoreType.DMA((13,)),
        ],
        compiler_params=pltpu.CompilerParams(
            collective_id=0, has_side_effects=True, vmem_limit_bytes=55125 * 1024
        ),
        name="v_cycle",
    )(intensities, labels)


def solution(mesh):
    return jax.shard_map(
        shards,
        mesh=mesh,
        in_specs=(P("gx", "gy", None), P("gx", "gy", None)),
        out_specs=P("gx", "gy", None),
        check_vma=False,
    )
```

```python
import jax
import jax.numpy as jnp
from jax import lax
from jax.experimental import pallas as pl
from jax.experimental.pallas import tpu as pltpu
from jax.sharding import PartitionSpec as P

COARSE_ITERS = 30

edge_beta = 3.0
seed_gamma = 4.0
base_mass = 0.1
damping = 0.7

MESH = pl.DeviceIdType.MESH
f32 = jnp.float32

BX, BY, BZ = 24, 8, 128
GX, GY = 16, 32

NEAR = [(dx, dy) for dx in (-1, 0, 1) for dy in (-1, 0, 1) if (dx, dy) != (0, 0)]
MIDDLE = [(dx, dy) for dx in (-1, 1, 0) for dy in (0, -1, 1, -2, 2) if (dx, dy) != (0, 0)]


def place(shape, axis):
    return lax.broadcasted_iota(jnp.int32, shape, axis)


def up(array, distance, axis):
    return pltpu.roll(array, array.shape[axis] - distance, axis)


def down(array, distance, axis):
    return pltpu.roll(array, distance, axis)


def odd(array, distance, axis):
    return (place(array.shape, axis) // distance) % 2 == 1


def high(array, distance, axis):
    return jnp.where(odd(array, distance, axis), array, up(array, distance, axis))


def low(array, distance, axis):
    return jnp.where(odd(array, distance, axis), down(array, distance, axis), array)


def pair(array, distance, axis):
    return array + jnp.where(
        odd(array, distance, axis), down(array, distance, axis), up(array, distance, axis)
    )


def halves(array):
    split = array.reshape((array.shape[0] // 2, 2) + array.shape[1:])
    return split[:, 0], split[:, 1]


def pair_x(array):
    first, second = halves(array)
    return first + second


def coarsen(operator, distance):
    px, py, my, pz, mass = operator
    next_px = jnp.concatenate([px[0:1], halves(px[1:])[1]], axis=0)
    next_px = pair(pair(next_px, distance, 1), distance, 2)
    next_py = high(pair(pair_x(py), distance, 2), distance, 1)
    next_my = low(pair(pair_x(my), distance, 2), distance, 1)
    next_pz = high(pair(pair_x(pz), distance, 1), distance, 2)
    next_mass = pair(pair(pair_x(mass), distance, 1), distance, 2)
    return next_px, next_py, next_my, next_pz, next_mass


def own_diagonal(operator, distance):
    px, py, my, pz, mass = operator
    return mass + px[1:] + px[:-1] + py + my + pz + down(pz, distance, 2)


def weight(upper, lower):
    gap = upper - lower
    return jnp.exp(gap * gap * (-edge_beta / (255.0 * 255.0)))


def step(source, first, count, weights, rhs, dist_y, dist_z, rows=None):
    v = source[pl.ds(first - 1, count + 2)]
    c = v[1:-1]
    near = [v[2:], v[:-2], up(c, dist_y, 1), down(c, dist_y, 1), up(c, dist_z, 2), down(c, dist_z, 2)]
    rows = c.shape[1] if rows is None else rows
    here = c[:, :rows]
    total = (1.0 - damping) * here + rhs[pl.ds(first, count), 0:rows, :]
    for w, n in zip(weights, near):
        total = total + w[pl.ds(first, count), 0:rows, :] * n[:, :rows]
    return here, total


def sweep(source, target, first, last, count, weights, rhs, dist_y, dist_z):
    def turn(index, carry):
        at = first + index * count
        _, total = step(source, at, count, weights, rhs, dist_y, dist_z)
        target[pl.ds(at, count)] = total
        return carry

    lax.fori_loop(0, (last + 1 - first) // count, turn, 0, unroll=True)


def normalise(px, px_before, py, my, pz, mz, mass, stores, at, count):
    diagonal = mass + px + px_before + py + my + pz + mz
    scale = damping / diagonal
    for store, value in zip(stores, (px, px_before, py, my, pz, mz)):
        store[pl.ds(at, count)] = value * scale
    return diagonal, scale


def kernel(
    ints, labels, out,
    ibuf, lbuf, w0, b0, d0, fine, va0, vb0,
    p1, b1p, b1, w1, d1, s1, va1, vb1,
    p2, x2, b2, w2, d2, s2, va2, vb2,
    o3, g1o, qo, g2o, o4, g1, q, g2, w3, b3, solved,
    local_sem, send_sem, recv_sem,
):
    gx, gy = lax.axis_index("gx"), lax.axis_index("gy")
    half, chip_y = gx // 8, gx % 8
    chip_z, chip_x, core = half * 4 + gy // 8, gy % 8 // 2, gy % 2
    groups = {}

    def device(dx, dy):
        return (lax.rem(gx + dx + GX, GX), lax.rem(gy + dy + GY, GY))

    def offset(k, size):
        return (size // 2 + (k + 1) // 2 * (1 - 2 * (k % 2))) % size

    def in_plane(k):
        return (half * 8 + (chip_y + offset(k // 2, 8)) % 8, gy - core + (core + k + 1) % 2)

    def in_column(k):
        z = (chip_z + offset(k // 4, 8)) % 8
        x = (chip_x + offset(k % 4, 4)) % 4
        return (z // 4 * 8 + chip_y, z % 4 * 8 + x * 2 + core)

    def send(source, target, which, to):
        pltpu.make_async_remote_copy(
            source, target, send_sem.at[which], recv_sem.at[which],
            device_id=to, device_id_type=MESH,
        ).start()

    def each(count, action):
        def turn(index, carry):
            action(index)
            return carry

        lax.fori_loop(0, count, turn, 0, unroll=True)

    def await_bytes(ref, sem):
        pltpu.make_async_copy(ref, ref, sem).wait()

    def arrived(which):
        await_bytes(groups[which], recv_sem.at[which])

    own = [
        pltpu.make_async_copy(ints, ibuf.at[4:28, 0:8], local_sem.at[0]),
        pltpu.make_async_copy(labels, lbuf.at[4:28, 0:8], local_sem.at[1]),
    ]
    for copy in own:
        copy.start()
    barrier = pltpu.get_barrier_semaphore()

    def greet(to):
        pl.semaphore_signal(barrier, inc=1, device_id=to, device_id_type=MESH)

    for dx, dy in MIDDLE:
        greet(device(dx, dy))
    each(15, lambda k: greet(in_plane(k)))
    each(31, lambda k: greet(in_column(k)))
    p2[:, 6:12, :] = jnp.ones((18, 6, BZ), f32)
    x2[:, 6:12, :] = jnp.zeros((18, 6, BZ), f32)
    pl.semaphore_wait(barrier, len(MIDDLE) + 15 + 31)

    for copy in own:
        copy.wait()

    def send_inputs(target, which, pairs, depth, corner_x, corner_y):
        for dx, dy in pairs:
            n, m = (corner_x, corner_y) if dx and dy else (depth, depth)
            sx, tx = {1: (28 - n, 4 - n), -1: (4, 28), 0: (4, 4)}[dx]
            sy, ty = {1: (8 - m, 16 - m), -1: (0, 8), 0: (0, 0)}[dy]
            nx, ny = n if dx else 24, m if dy else 8
            send(
                target.at[sx : sx + nx, sy : sy + ny], target.at[tx : tx + nx, ty : ty + ny],
                which, device(dx, dy),
            )

    aside = [d for d in NEAR if d[0] == 0]
    ahead = [(1, 0), (-1, 0), (1, 1), (1, -1), (-1, 1), (-1, -1)]
    send_inputs(ibuf, 11, ahead, 4, 3, 4)
    send_inputs(lbuf, 12, ahead, 3, 2, 2)
    send_inputs(ibuf, 0, aside, 4, 3, 4)
    send_inputs(lbuf, 1, aside, 3, 2, 2)
    groups[0], groups[1] = ibuf.at[0:12], lbuf.at[0:9]
    groups[11], groups[12] = ibuf.at[0:7], lbuf.at[0:4]
    arrived(0)
    arrived(1)

    def fine_operator(at, count):
        wide = ibuf[pl.ds(at - 1, count + 2)].astype(f32)
        lab = lbuf[pl.ds(at, count)]
        c = wide[1:-1]
        px = weight(wide[1:], wide[:-1])
        gone_x = gx * BX + (at - 5) + place(px.shape, 0)
        px = jnp.where((gone_x == GX * BX - 1) | (gone_x == -1), 0.0, px)
        row = place(c.shape, 1)
        gone_y = gy * BY + jnp.where(row >= 12, row - 16, row)
        py = jnp.where((gone_y == GY * BY - 1) | (gone_y == -1), 0.0, weight(up(c, 1, 1), c))
        my = down(py, 1, 1)
        pz = jnp.where(place(c.shape, 2) == BZ - 1, 0.0, weight(up(c, 1, 2), c))
        mz = down(pz, 1, 2)
        mass = base_mass + jnp.where(lab > 0, seed_gamma, 0.0)
        diagonal, scale = normalise(px[1:], px[:-1], py, my, pz, mz, mass, w0, at, count)
        b0[pl.ds(at, count)] = jnp.where(lab == 1, seed_gamma, 0.0) * scale
        d0[pl.ds(at, count)] = diagonal[:, 0:8] * (1.0 / damping)
        for slot, value in enumerate((px[1:], py, my, pz, mass)):
            fine[slot, pl.ds(at, count)] = value[:, 0:8]

    def level_1(first, last):
        at, end = 4 + 2 * first, 6 + 2 * last
        return coarsen((fine[0, at - 1 : end], *(fine[slot, at:end] for slot in range(1, 5))), 1)

    def packed_1(operator):
        px, py, _, pz, mass = operator
        ybit, zbit = odd(py, 1, 1), odd(py, 1, 2)
        return jnp.where(ybit, jnp.where(zbit, mass, pz), jnp.where(zbit, py, px[1:]))

    def send_1(ref, which, near, whole, corners, ends):
        for dx, dy in MIDDLE:
            if abs(dy) == 2:
                parts = [(*{1: (4, 20), -1: (0, 16)}[dy // 2], 4, corners[2])]
            elif dx and dy and corners[0] == corners[1]:
                parts = [(0, {1: 24, -1: 8}[dy], 8, corners[0])]
            elif dx and dy:
                close, far = {1: ((4, 28), (0, 24)), -1: ((0, 8), (4, 12))}[dy]
                parts = [(*close, 4, corners[0]), (*far, 4, corners[1])]
            else:
                parts = [(0, {0: 0, 1: 24, -1: 8}[dy], 8, near)]
            for sy, ty, ny, n in parts:
                nx = n - ends if dx else whole - 2 * ends
                sx = near + {1: whole - n, -1: ends, 0: ends}[dx]
                tx = {1: near - n, -1: near + whole + ends, 0: near + ends}[dx]
                if nx > 0:
                    send(
                        ref.at[sx : sx + nx, sy : sy + ny], ref.at[tx : tx + nx, ty : ty + ny],
                        which, device(dx, dy),
                    )

    for at in (5, 16):
        fine_operator(at, 11)
    inner = level_1(1, 10)
    p1[7:17, 0:8, :] = packed_1(inner)
    send_1(p1, 2, 6, 12, (5, 3, 1), 1)
    groups[2] = p1.at[0:13]
    sweep(b0, va0, 6, 25, 4, w0, b0, 1, 1)
    s1[1:11] = damping / own_diagonal(inner, 2)

    def residual_0(index):
        at = 4 + 6 * index
        here, total = step(va0, at, 6, w0, b0, 1, 1, 8)
        r = pair_x(d0[pl.ds(at, 6)] * (total - here))
        r = pair(pair(r, 1, 1), 1, 2) * s1[pl.ds(3 * index, 3)]
        ybit, zbit = odd(r[0:1], 1, 1), odd(r[0:1], 1, 2)
        b1p[pl.ds(4 + index, 1), 0:8, :] = jnp.where(zbit, jnp.where(ybit, r[2:3], r[1:2]), r[0:1])

    residual_0(1)
    residual_0(2)
    arrived(11)
    arrived(12)
    fine_operator(1, 4)
    fine_operator(27, 4)

    lower, upper = level_1(0, 0), level_1(11, 11)
    b1p[3:4, 0:8, :] = packed_1(lower)
    b1p[8:9, 0:8, :] = packed_1(upper)
    s1[0:1] = damping / own_diagonal(lower, 2)
    s1[11:12] = damping / own_diagonal(upper, 2)

    sweep(b0, va0, 2, 5, 4, w0, b0, 1, 1)
    sweep(b0, va0, 26, 29, 4, w0, b0, 1, 1)

    residual_0(0)
    residual_0(3)
    send_1(b1p, 3, 3, 6, (3, 3, 2), 0)
    groups[3] = b1p.at[0:10]

    op1 = (
        jnp.concatenate([lower[0][0:1], inner[0], upper[0][1:2]], axis=0),
        *(jnp.concatenate(parts, axis=0) for parts in zip(lower[1:], inner[1:], upper[1:])),
    )
    op2 = coarsen(op1, 2)
    px, py, _, pz, mass = op2
    slot = place(py.shape, 2) % 4
    packed = jnp.where(slot == 0, px[1:], jnp.where(slot == 1, py, jnp.where(slot == 2, pz, mass)))
    p2[6:12, 0:2, :] = jnp.where(place(packed.shape, 1) == 0, packed, up(packed, 3, 1))[:, 0:2]

    def send_2(ref, which):
        for dx, dy in MIDDLE:
            n = 6 if dx == 0 else 2 if abs(dy) == 2 else 4
            sx = 12 - n if dx == 1 else 6
            tx = {1: 6 - n, -1: 12, 0: 6}[dx]
            ty = -2 * dy % 16
            send(ref.at[sx : sx + n, 0:2], ref.at[tx : tx + n, ty : ty + 2], which, device(dx, dy))
        groups[which] = ref.at[0:7]

    op3 = coarsen(op2, 4)
    s3 = damping / own_diagonal(op3, 8)
    px, py, _, pz, mass = op3
    for index, value in enumerate((px[1:], py, pz, mass)):
        o3[3 * index : 3 * index + 3] = value

    def gather_plane(source, target, which):
        seat = core * 8 + chip_y
        target[:, pl.ds(seat, 1), :] = source[:, 0:1, :]
        each(15, lambda k: send(source.at[:, 0:1], target.at[:, pl.ds(seat, 1)], which, in_plane(k)))
        groups[which] = target.at[:, 0:15]

    def merge(source, target, kinds):
        rows = source[...]
        rows = jnp.where(place(rows.shape, 2) % 8 == place(rows.shape, 1) % 8, rows, 0.0)
        rows = rows.reshape(3 * kinds * 2, 8, BZ)
        for distance in (1, 2, 4):
            rows = rows + up(rows, distance, 1)
        target[...] = rows.reshape(kinds, 3, 2, 8, BZ)

    def gather_column(source, target, which, kinds):
        piece = source.at[kinds, :, :, 0:1]
        seat = target.at[kinds, half, :, pl.ds(gy % 4 // 2 * 2, 2), pl.ds(gy // 4, 1)]
        each(31, lambda k: send(piece, seat, which, in_column(k)))
        pltpu.make_async_copy(piece, seat, recv_sem.at[which]).start()

    gather_plane(o3, g1o, 6)
    send_2(p2, 4)

    arrived(2)

    def weights_1(at, count):
        packed = p1[at - 1 : at + count]
        even_z, odd_z = low(packed, 1, 2), high(packed[1:], 1, 2)
        px, pz = low(even_z, 1, 1), high(even_z[1:], 1, 1)
        py, mass = low(odd_z, 1, 1), high(odd_z, 1, 1)
        diagonal, _ = normalise(px[1:], px[:-1], py, down(py, 2, 1), pz, down(pz, 2, 2), mass, w1, at, count)
        d1[at : at + count] = diagonal * (1.0 / damping)

    for at, count in ((1, 4), (8, 3), (11, 3), (14, 3), (20, 3)):
        weights_1(at, count)
    arrived(6)
    merge(g1o, qo, 4)
    half_kinds = pl.ds(2 * core, 2)
    gather_column(qo, g2o, 7, half_kinds)
    groups[7] = g2o.at[0:2]
    arrived(3)
    for plane, end in ((5, 2), (6, 3), (17, 8), (18, 9)):
        p1[plane] = b1p[end]
    for at in (5, 17):
        weights_1(at, 3)
    for index, plane in enumerate((0, 1, 4, 5, 6, 7, 10, 11)):
        packed = b1p[plane : plane + 1]
        odd_z = high(packed, 1, 2)
        b1[3 * index : 3 * index + 1] = low(packed, 1, 2)
        b1[3 * index + 1 : 3 * index + 2] = low(odd_z, 1, 1)
        b1[3 * index + 2 : 3 * index + 3] = high(odd_z, 1, 1)
    sweep(b1, va1, 1, 22, 2, w1, b1, 2, 2)

    def residual_1(index, carry):
        at = 2 + 4 * index
        here, total = step(va1, at, 4, w1, b1, 2, 2)
        r = pair_x(d1[pl.ds(at, 4)] * (total - here))
        r = pair(pair(r, 2, 1), 2, 2)
        mine, after, before = r[:, 0:8], r[:, 8:16], r[:, 24:32]
        row = place(mine.shape, 1)
        first = jnp.where(row < 2, jnp.where(row == 0, mine, up(mine, 3, 1)), jnp.where(row == 2, down(after, 2, 1), up(after, 1, 1)))
        last = jnp.where(row == 7, down(before, 3, 1), up(before, 2, 1))
        to = pl.ds(4 + 2 * index, 2)
        b2[to, 0:8, :] = first
        b2[to, 8:16, :] = last
        return carry

    lax.fori_loop(0, 5, residual_1, 0, unroll=True)

    arrived(4)

    def weights_2(index, carry):
        at = 1 + 4 * index
        packed = p2[pl.ds(at - 1, 5)]
        even_z, odd_z = low(packed, 1, 2), high(packed[1:], 1, 2)
        px, pz = low(even_z, 2, 2), high(even_z[1:], 2, 2)
        py, mass = low(odd_z, 2, 2), high(odd_z, 2, 2)
        diagonal, scale = normalise(px[1:], px[:-1], py, down(py, 1, 1), pz, down(pz, 4, 2), mass, w2, at, 4)
        d2[pl.ds(at, 4)] = diagonal * (1.0 / damping)
        s2[pl.ds(at, 4)] = scale
        return carry

    lax.fori_loop(0, 4, weights_2, 0, unroll=True)
    b2[4:14] = b2[4:14] * s2[4:14]

    sweep(b2, va2, 5, 12, 4, w2, b2, 1, 4)
    here, total = step(va2, 6, 6, w2, b2, 1, 4, 8)
    r = pair_x(d2[6:12, 0:8, :] * (total - here))
    r = pair(pair(r, 1, 1), 4, 2)
    o4[...] = r * s3
    gather_plane(o4, g1, 8)

    zbit = odd(here[:, 0:2], 1, 2)
    x2[6:12, 0:2, :] = jnp.where(zbit, b2[6:12, 0:2, :], here[:, 0:2])
    send_2(x2, 5)

    arrived(8)
    merge(g1, q, 1)
    gather_column(q, g2, 9, pl.ds(0, 1))
    groups[9] = g2

    arrived(7)
    send(g2o.at[half_kinds], g2o.at[half_kinds], 10, (gx, gy + 1 - 2 * core))
    groups[10] = g2o.at[0:2]
    arrived(5)
    b2[...] = high(x2[...], 1, 2)
    va2[...] = low(x2[...], 1, 2)

    whole = (3, 4, 2, 8, BZ)

    def lanes(v, shift):
        return pltpu.roll(v.reshape(-1, 8, BZ), shift, 2).reshape(v.shape)

    def rows(v, shift):
        return pltpu.roll(v.reshape(-1, 8, BZ), shift, 1).reshape(v.shape)

    def spread(v):
        second = odd(v[0], 8, 3)
        return jnp.stack(
            [jnp.where(second, lanes(v[1], 8), v[0]), jnp.where(second, v[1], lanes(v[0], BZ - 8))],
            axis=2,
        )

    def around(v):
        return (
            jnp.concatenate([v[1:], lanes(v[:1], BZ - 1)], axis=0),
            jnp.concatenate([lanes(v[2:], 1), v[:2]], axis=0),
            jnp.concatenate([v[:, 1:], rows(v[:, :1], 7)], axis=1),
            jnp.concatenate([rows(v[:, 3:], 1), v[:, :3]], axis=1),
            jnp.concatenate([v[:, :, 1:], lanes(v[:, :, :1], BZ - 16)], axis=2),
            jnp.concatenate([lanes(v[:, :, 1:], 16), v[:, :, :1]], axis=2),
        )

    arrived(10)
    px, py, pz, mass = [spread(g2o[k]) for k in range(4)]
    mx, my, mz = around(px)[1], around(py)[3], around(pz)[5]
    scale = damping / (mass + px + mx + py + my + pz + mz)
    for index, value in enumerate((px, mx, py, my, pz, mz)):
        w3[index] = value * scale
    arrived(9)
    b3[...] = spread(g2[0])

    def solve(index, v):
        total = (1.0 - damping) * v + b3[...]
        for k, n in enumerate(around(v)):
            total = total + w3[k] * n
        return total

    solved[...] = lax.fori_loop(1, COARSE_ITERS, solve, b3[...], unroll=True)

    row = (place((16, BZ), 0) // 2 + 2) % 8
    slot = place((16, BZ), 1) % 16
    for j in range(-2, 5):
        at = (3 * gx + j + 48) % 48
        tiles = []
        for z_low in range(2):
            tile = jnp.zeros((16, BZ), f32)
            for k in range(-2, 3):
                y = (gy + k + GY) % GY
                line = solved[pl.ds(at % 3, 1), pl.ds(y % 4, 1), z_low, pl.ds(y // 4, 1), :]
                tile = jnp.where(row == k + 2, line.reshape(1, BZ), tile)
            tiles.append(pair(jnp.where(slot == at // 3, tile, 0.0), 8, 1))
        tile = jnp.where(slot >= 8, tiles[1], tiles[0])
        tile = pair(pair(pair(tile, 1, 1), 2, 1), 4, 1)
        va2[6 + 2 * j : 8 + 2 * j] = va2[6 + 2 * j : 8 + 2 * j] + tile[None]
    sweep(va2, vb2, 3, 14, 4, w2, b2, 1, 4)
    sweep(vb2, va2, 4, 13, 5, w2, b2, 1, 4)

    second = place((1, 8, BZ), 1) >= 4

    def correct_1(index, carry):
        for rows, first in ((0, 0), (8, 2), (24, 14)):
            a = va2[pl.ds(4 + index, 1), first : first + 1, :]
            b = va2[pl.ds(4 + index, 1), first + 1 : first + 2, :]
            at = pl.ds(2 + 2 * index, 2)
            va1[at, rows : rows + 8, :] = va1[at, rows : rows + 8, :] + jnp.where(second, b, a)
        return carry

    lax.fori_loop(0, 10, correct_1, 0, unroll=True)
    sweep(va1, vb1, 4, 19, 2, w1, b1, 2, 2)
    sweep(vb1, va1, 5, 18, 2, w1, b1, 2, 2)

    def correct_0(index, carry):
        at = pl.ds(2 + 2 * index, 2)
        coarse = va1[pl.ds(5 + index, 1)]
        va0[at, 0:8, :] = va0[at, 0:8, :] + coarse[:, 0:8]
        va0[at, 8:16, :] = va0[at, 8:16, :] + jnp.where(second, coarse[:, 24:32], coarse[:, 8:16])
        return carry

    lax.fori_loop(0, 14, correct_0, 0, unroll=True)
    sweep(va0, vb0, 2, 29, 4, w0, b0, 1, 1)

    for at in (0, 8, 16):
        _, total = step(vb0, 4 + at, 8, w0, b0, 1, 1, 8)
        out[at : at + 8] = total

    for which in (0, 1, 2, 3, 4, 5, 6, 8, 10, 11, 12):
        await_bytes(groups[which], send_sem.at[which])
    await_bytes(p1.at[0:12, 0:31], send_sem.at[7])
    await_bytes(p1.at[0:6, 0:31], send_sem.at[9])


def shards(intensities, labels):
    def vmem(*shape, dtype=f32):
        return pltpu.VMEM(shape, dtype)

    zero, one, two = (32, 16, BZ), (24, 32, BZ), (18, 16, BZ)
    return pl.pallas_call(
        kernel,
        out_shape=jax.ShapeDtypeStruct((BX, BY, BZ), f32),
        in_specs=[pl.BlockSpec(memory_space=pltpu.HBM)] * 2,
        out_specs=pl.BlockSpec(memory_space=pltpu.VMEM),
        scratch_shapes=[
            vmem(*zero, dtype=jnp.int32), vmem(*zero, dtype=jnp.int32),
            [vmem(*zero)] * 6, vmem(*zero), vmem(32, 8, BZ), vmem(5, 32, 8, BZ),
            vmem(*zero), vmem(*zero),
            vmem(*one), vmem(12, 32, BZ), vmem(*one), [vmem(*one)] * 6, vmem(*one), vmem(12, 8, BZ),
            vmem(*one), vmem(*one),
            vmem(*two), vmem(*two), vmem(*two), [vmem(*two)] * 6, vmem(*two), vmem(*two),
            vmem(*two), vmem(*two),
            vmem(12, 8, BZ), vmem(12, 16, BZ), vmem(4, 3, 2, 8, BZ), vmem(4, 2, 3, 4, 8, BZ),
            vmem(3, 8, BZ), vmem(3, 16, BZ), vmem(1, 3, 2, 8, BZ), vmem(1, 2, 3, 4, 8, BZ),
            vmem(6, 3, 4, 2, 8, BZ), vmem(3, 4, 2, 8, BZ), vmem(3, 4, 2, 8, BZ),
            pltpu.SemaphoreType.DMA((2,)),
            pltpu.SemaphoreType.DMA((13,)),
            pltpu.SemaphoreType.DMA((13,)),
        ],
        compiler_params=pltpu.CompilerParams(
            collective_id=0, has_side_effects=True, vmem_limit_bytes=55125 * 1024
        ),
        name="v_cycle",
    )(intensities, labels)


def solution(mesh):
    return jax.shard_map(
        shards,
        mesh=mesh,
        in_specs=(P("gx", "gy", None), P("gx", "gy", None)),
        out_specs=P("gx", "gy", None),
        check_vma=False,
    )
```
